128 devices in a mesh: ctx: 16 (over x, y), chan: 8 (over z, core).
Axes of the slice: x: 4, y: 4, z: 4, core: 2. Of those that a mesh axis runs over, the one named last changes fastest.
Arguments:
- projections: bfloat16 [3, 256, 65536], P(None, 'chan', 'ctx'), may hold values from -6 to 6
- short_taps: float32 [3, 3, 256], P(None, None, 'chan'), may hold values from -1 to 1
- long_filter: bfloat16 [256, 65536], P('chan', 'ctx'), may hold values from -2 to 2
Outputs:
- gated: bfloat16 [256, 65536], P('chan', 'ctx')
The draws below stay inside these ranges and needn't reach their ends.
All inputs are finite; a program needn't handle non-finite values.
Results may differ from the reference program's by a relative error of at most 0.014.
Values may be sent and summed in bfloat16 or wider, within the bound.
A program may use at most 64 MiB of HBM per device.

```python
import math
import jax
import jax.numpy as jnp
from jax import lax

CHANNELS = 256
TOKENS = 65536


def draw_short_taps(key, part):
    key = jax.random.fold_in(key, 11)
    sign_key, lead_key, rest_key = jax.random.split(key, 3)
    signs = jax.random.rademacher(sign_key, (3, 1, CHANNELS), jnp.float32)
    lead = signs * jax.random.uniform(lead_key, (3, 1, CHANNELS), jnp.float32, 0.75, 1.0)
    rest = jax.random.uniform(rest_key, (3, 2, CHANNELS), jnp.float32, -0.5, 0.5)
    return jnp.concatenate([lead, rest], axis=1)


def draw_long_filter(key, part):
    key = jax.random.fold_in(key, 7)
    rate_key, noise_key, floor_key = jax.random.split(key, 3)
    low = math.log(1.0 / (4.0 * TOKENS))
    log_rate = jax.random.uniform(rate_key, (CHANNELS, 1), jnp.float32, low, math.log(1.0 / 40.0))
    noise = jnp.clip(jax.random.normal(noise_key, (CHANNELS, TOKENS), jnp.float32), -6.0, 6.0)
    floor_noise = jnp.clip(jax.random.normal(floor_key, (CHANNELS, TOKENS), jnp.float32), -6.0, 6.0)
    decay = jnp.exp(log_rate)
    places = jnp.arange(TOKENS, dtype=jnp.float32)[None, :]
    leading = noise * jnp.sqrt(2.0 * decay + 1.0 / TOKENS) * jnp.exp(-decay * places)
    lasting = floor_noise * math.sqrt(0.4 / TOKENS) * jnp.exp(-places / TOKENS)
    return (leading + lasting).astype(jnp.bfloat16)


def shard_levels(own_key, extent, cuts, smallest, largest):
    factor_of = 1.0
    for axis_at, parts in cuts:
        draws = jax.random.uniform(jax.random.fold_in(jax.random.fold_in(own_key, 6), axis_at), (parts,), jnp.float32, smallest / len(cuts), largest / len(cuts))
        factor_of = factor_of * jnp.repeat(jnp.exp(draws), extent[axis_at] // parts).reshape((-1,) + (1,) * (len(extent) - 1 - axis_at))
    return factor_of


def normal_values(own_key, extent, scale, most, cuts=(), kind=jnp.bfloat16):
    values = scale * jax.random.normal(own_key, extent, jnp.float32)
    if cuts:
        values = values * shard_levels(own_key, extent, cuts, -0.22, 0.18)
    return jnp.clip(values, -most, most).astype(kind)


def setup_inputs(seed: int = 0) -> dict:
    streams_of = jax.random.split(jax.random.key(seed), 4)
    projections = normal_values(streams_of[0], (3, CHANNELS, TOKENS), 1.0, 6.0, ((1, 8), (2, 16)))
    short_taps = draw_short_taps(jax.random.fold_in(streams_of[3], 71), 0)
    long_filter = draw_long_filter(jax.random.fold_in(streams_of[3], 71), 0)
    return dict(projections=projections, short_taps=short_taps, long_filter=long_filter)


def reference(projections, short_taps, long_filter):
    values = projections.astype(jnp.float32)
    padded = jnp.pad(values, ((0, 0), (0, 0), (2, 0)))
    short = short_taps[:, 0, :, None] * values + short_taps[:, 1, :, None] * padded[:, :, 1:-1] + short_taps[:, 2, :, None] * padded[:, :, :-2]
    mixed = (short[1] * short[2]).astype(jnp.bfloat16)
    mixed = lax.optimization_barrier(mixed).astype(jnp.float32)
    length = 2 * TOKENS
    spectrum = jnp.fft.rfft(mixed, n=length, axis=-1) * jnp.fft.rfft(long_filter.astype(jnp.float32), n=length, axis=-1)
    convolved = jnp.fft.irfft(spectrum, n=length, axis=-1)[:, :TOKENS]
    return (short[0] * convolved).astype(jnp.bfloat16)
```

```python
import functools

import jax
import jax.numpy as jnp
import ml_dtypes
import numpy as np
from jax import lax
from jax.experimental import pallas as pl
from jax.experimental.pallas import tpu as pltpu
from jax.sharding import PartitionSpec as P

MESH = pl.DeviceIdType.MESH
LANES = 128
SIDE = 256
TOTAL = SIDE * SIDE


def tables():
    k = np.arange(SIDE, dtype=np.float64)

    def cis(a, b, length):
        angle = 2.0 * np.pi * np.fmod(a[:, None] * b[None, :], length) / length
        return np.cos(angle), np.sin(angle)

    cos, sin = cis(k + 0.25, k, SIDE)
    rows = np.concatenate([cos, -sin], axis=0)
    back_rows = np.concatenate([cos.T, -sin.T], axis=1) / TOTAL
    twist = np.stack(cis(k + 0.25, k, TOTAL))
    cos, sin = cis(k, k, SIDE)
    columns = np.block([[cos, -sin], [sin, cos]])
    back_columns = np.block([[cos, sin], [-sin, cos]])
    bf16 = ml_dtypes.bfloat16
    return (
        rows.astype(bf16),
        columns.astype(bf16),
        back_columns.astype(bf16),
        back_rows.astype(bf16),
        twist.astype(np.float32),
    )


def kernel(
    n,
    proj_hbm, filt_hbm, taps_ref, rows_hbm, cols_hbm, bcols_hbm, brows_hbm, twist_hbm,
    out_hbm,
    proj, filt, rows, cols, bcols, brows, twist, gate, stage,
    h_out, x_out, y_out, h_in, x_in, y_in, h_freq, back, out,
    load_sem, halo_send, halo_recv, h_send, h_recv, x_send, x_recv, y_send, y_recv, own_sem, out_sem,
):
    f32, bf16 = jnp.float32, jnp.bfloat16
    me = lax.axis_index("ctx")
    width = filt.shape[1]
    tiles = width // LANES
    half = filt.shape[0] // 2

    loads = [
        pltpu.make_async_copy(filt_hbm, filt, load_sem.at[0]),
        pltpu.make_async_copy(proj_hbm, proj.at[:, :, pl.ds(LANES, width)], load_sem.at[1]),
        pltpu.make_async_copy(rows_hbm, rows, load_sem.at[2]),
        pltpu.make_async_copy(twist_hbm, twist, load_sem.at[3]),
        pltpu.make_async_copy(cols_hbm, cols, load_sem.at[4]),
        pltpu.make_async_copy(bcols_hbm, bcols, load_sem.at[5]),
        pltpu.make_async_copy(brows_hbm, brows, load_sem.at[6]),
    ]
    for load in loads:
        load.start()

    barrier = pltpu.get_barrier_semaphore()

    def greet(step, carry):
        peer = lax.rem(me + step, n)
        pl.semaphore_signal(barrier, inc=1, device_id={"ctx": peer}, device_id_type=MESH)
        return carry

    lax.fori_loop(1, n, greet, 0)

    def block(ref, at):
        return ref.at[pl.ds(pl.multiple_of(at * 16, 16), 16)]

    def send_all(source, target, send_sem, recv_sem, own):
        def send(step, carry):
            peer = lax.rem(me + step, n)
            pltpu.make_async_remote_copy(
                src_ref=block(source, peer), dst_ref=block(target, me), send_sem=send_sem, recv_sem=recv_sem,
                device_id={"ctx": peer}, device_id_type=MESH,
            ).start()
            return carry

        lax.fori_loop(1, n, send, 0)
        pltpu.make_async_copy(block(source, me), block(target, me), own).start()

    def others(ref, send_sem, recv_sem):
        part = ref.at[pl.ds(0, 16 * (n - 1))]
        return pltpu.make_async_remote_copy(
            src_ref=part, dst_ref=part, send_sem=send_sem, recv_sem=recv_sem, device_id={"ctx": me}, device_id_type=MESH
        )

    def arrived(target, recv_sem, own):
        others(target, recv_sem, recv_sem).wait_recv()
        pltpu.make_async_copy(block(target, me), block(target, me), own).wait()

    def spread(value, group, tile_row, parity):
        stage[parity, pl.ds(group * 8 * 16 + tile_row, 8, stride=16), :] = value

    def gathered(target):
        target[:, 0:LANES] = stage[0].astype(bf16)
        target[:, LANES:SIDE] = stage[1].astype(bf16)

    loads[0].wait()

    def place_filter(j):
        def tile_pair(row, carry):
            for parity in range(2):
                at = pl.multiple_of((2 * row + parity) * LANES, LANES)
                value = filt[half * j : half * (j + 1), pl.ds(at, LANES)].astype(f32)
                for group in range(2):
                    spread(value[8 * group : 8 * group + 8], group, row, parity)
            return carry

        lax.fori_loop(0, tiles // 2, tile_pair, 0)
        gathered(h_out.at[j])

    place_filter(0)
    loads[1].wait()
    pl.semaphore_wait(barrier, n - 1)

    halo = pltpu.make_async_remote_copy(
        src_ref=proj.at[:, :, pl.ds(width, LANES)], dst_ref=proj.at[:, :, pl.ds(0, LANES)],
        send_sem=halo_send, recv_sem=halo_recv, device_id={"ctx": lax.rem(me + 1, n)}, device_id_type=MESH,
    )

    @pl.when(me < n - 1)
    def _():
        halo.start()

    @pl.when(me == 0)
    def _():
        proj[:, :, 0:LANES] = jnp.zeros((3, 2 * half, LANES), bf16)

    send_all(h_out.at[0], h_in.at[0], h_send.at[0], h_recv.at[0], own_sem.at[0])
    place_filter(1)
    send_all(h_out.at[1], h_in.at[1], h_send.at[1], h_recv.at[1], own_sem.at[1])

    diagonal = lax.broadcasted_iota(jnp.int32, (half, 2 * half), 0)
    along = lax.broadcasted_iota(jnp.int32, (half, 2 * half), 1)
    lane = lax.broadcasted_iota(jnp.int32, (half, LANES), 1)

    def tap(stream, lag, j):
        row = jnp.broadcast_to(taps_ref[stream, lag, :][None, :], (half, 2 * half))
        column = jnp.sum(jnp.where(along == diagonal + half * j, row, 0.0), axis=1, keepdims=True)
        return jnp.broadcast_to(column, (half, LANES))

    def tile_of(stream, at, j):
        start = pl.multiple_of(at * LANES, LANES)
        value = proj[stream, half * j : half * (j + 1), pl.ds(start, LANES)].astype(f32)
        return value, pltpu.roll(value, 1, 1), pltpu.roll(value, 2, 1)

    def short(taps, now, before):
        one = jnp.where(lane < 1, before[1], now[1])
        two = jnp.where(lane < 2, before[2], now[2])
        return taps[0] * now[0] + taps[1] * one + taps[2] * two

    def place_mixed(j):
        taps = [[tap(stream, lag, j) for lag in range(3)] for stream in (1, 2)]

        def one_tile(row, parity, now):
            before = [tile_of(stream, 2 * row + parity, j) for stream in (1, 2)]
            value = short(taps[0], now[0], before[0]) * short(taps[1], now[1], before[1])
            for group in range(2):
                spread(value[8 * group : 8 * group + 8], group, row, parity)
            return before

        def tile_pair(step, now):
            row = tiles // 2 - 1 - step
            return one_tile(row, 0, one_tile(row, 1, now))

        now = [tile_of(stream, tiles, j) for stream in (1, 2)]
        now = lax.fori_loop(0, tiles // 2 - 1, tile_pair, now)
        now = one_tile(0, 1, now)
        if j == 0:
            @pl.when(me > 0)
            def _():
                halo.wait_recv()
        one_tile(0, 0, now)
        gathered(x_out.at[j])
        send_all(x_out.at[j], x_in.at[j], x_send.at[j], x_recv.at[j], own_sem.at[2 + j])

    place_mixed(0)
    place_mixed(1)

    def place_gate(j):
        taps = [tap(0, lag, j) for lag in range(3)]

        def tile(at, before):
            now = tile_of(0, at + 1, j)
            gate[half * j : half * (j + 1), pl.ds(pl.multiple_of(at * LANES, LANES), LANES)] = short(taps, now, before)
            return now

        lax.fori_loop(0, tiles, tile, tile_of(0, 0, j))

    place_gate(0)
    place_gate(1)
    for load in loads[2:]:
        load.wait()

    def dot(a, b):
        return jnp.dot(a, b, preferred_element_type=f32)

    def forward(ref):
        part = dot(rows[...], ref[...])
        real, imag = part[:SIDE], part[SIDE:]
        cos, sin = twist[0], twist[1]
        turned = jnp.concatenate(
            [(real * cos + imag * sin).astype(bf16), (imag * cos - real * sin).astype(bf16)], axis=1
        )
        return dot(turned, cols[...])

    for j in range(2):
        arrived(h_in.at[j], h_recv.at[j], own_sem.at[j])
        h_freq[j] = forward(h_in.at[j])

    for j in range(2):
        arrived(x_in.at[j], x_recv.at[j], own_sem.at[2 + j])
        freq = forward(x_in.at[j])
        x_re, x_im = freq[:, :SIDE], freq[:, SIDE:]
        h_re, h_im = h_freq[j, :, :SIDE], h_freq[j, :, SIDE:]
        product = jnp.concatenate(
            [(x_re * h_re - x_im * h_im).astype(bf16), (x_re * h_im + x_im * h_re).astype(bf16)], axis=1
        )
        part = dot(product, bcols[...])
        real, imag = part[:, :SIDE], part[:, SIDE:]
        cos, sin = twist[0], twist[1]
        back[:SIDE] = (real * cos - imag * sin).astype(bf16)
        back[SIDE:] = (imag * cos + real * sin).astype(bf16)
        y_out[j] = dot(brows[...], back[...]).astype(bf16)
        send_all(y_out.at[j], y_in.at[j], y_send.at[j], y_recv.at[j], own_sem.at[4 + j])

    writes = []
    for j in range(2):
        arrived(y_in.at[j], y_recv.at[j], own_sem.at[4 + j])
        stage[0] = y_in[j, :, 0:LANES].astype(f32)
        stage[1] = y_in[j, :, LANES:SIDE].astype(f32)

        def tile_pair(row, carry):
            for parity in range(2):
                at = pl.multiple_of((2 * row + parity) * LANES, LANES)
                value = jnp.concatenate(
                    [stage[parity, pl.ds(group * 8 * 16 + row, 8, stride=16), :] for group in range(2)], axis=0
                )
                value = value * gate[half * j : half * (j + 1), pl.ds(at, LANES)]
                out[half * j : half * (j + 1), pl.ds(at, LANES)] = value.astype(bf16)
            return carry

        lax.fori_loop(0, tiles // 2, tile_pair, 0)
        channels = pl.ds(half * j, half)
        write = pltpu.make_async_copy(out.at[channels], out_hbm.at[channels], out_sem.at[j])
        write.start()
        writes.append(write)

    @pl.when(me < n - 1)
    def _():
        halo.wait_send()

    for j in range(2):
        others(h_out.at[j], h_send.at[j], h_send.at[j]).wait_send()
        others(x_out.at[j], x_send.at[j], x_send.at[j]).wait_send()
        others(y_out.at[j], y_send.at[j], y_send.at[j]).wait_send()
    for write in writes:
        write.wait()


def shards(n, projections, short_taps, long_filter):
    channels, width = long_filter.shape
    f32, bf16 = jnp.float32, jnp.bfloat16
    anywhere = pl.BlockSpec(memory_space=pl.ANY)
    square = pltpu.VMEM((2, SIDE, SIDE), bf16)
    pair = pltpu.SemaphoreType.DMA((2,))
    one = pltpu.SemaphoreType.DMA
    return pl.pallas_call(
        functools.partial(kernel, n),
        out_shape=jax.ShapeDtypeStruct((channels, width), bf16),
        in_specs=[anywhere, anywhere, pl.BlockSpec(memory_space=pltpu.VMEM)] + [anywhere] * 5,
        out_specs=anywhere,
        scratch_shapes=[
            pltpu.VMEM((3, channels, LANES + width), bf16),
            pltpu.VMEM((channels, width), bf16),
            pltpu.VMEM((2 * SIDE, SIDE), bf16),
            pltpu.VMEM((2 * SIDE, 2 * SIDE), bf16),
            pltpu.VMEM((2 * SIDE, 2 * SIDE), bf16),
            pltpu.VMEM((SIDE, 2 * SIDE), bf16),
            pltpu.VMEM((2, SIDE, SIDE), f32),
            pltpu.VMEM((channels, width), f32),
            pltpu.VMEM((2, SIDE, LANES), f32),
            square, square, square, square, square, square,
            pltpu.VMEM((2, SIDE, 2 * SIDE), f32),
            pltpu.VMEM((2 * SIDE, SIDE), bf16),
            pltpu.VMEM((channels, width), bf16),
            pltpu.SemaphoreType.DMA((7,)),
            one, one, pair, pair, pair, pair, pair, pair,
            pltpu.SemaphoreType.DMA((6,)),
            pair,
        ],
        compiler_params=pltpu.CompilerParams(
            collective_id=0, has_side_effects=True, vmem_limit_bytes=32 * 1024 * 1024
        ),
        name="long_convolution",
    )(projections, long_filter, short_taps, *(jnp.asarray(t) for t in tables()))


def solution(mesh):
    in_specs = (P(None, "chan", "ctx"), P(None, None, "chan"), P("chan", "ctx"))
    return jax.shard_map(
        functools.partial(shards, mesh.shape["ctx"]),
        mesh=mesh, in_specs=in_specs, out_specs=P("chan", "ctx"), check_vma=False,
    )
```

```python
import functools

import jax
import jax.numpy as jnp
import ml_dtypes
import numpy as np
from jax import lax
from jax.experimental import pallas as pl
from jax.experimental.pallas import tpu as pltpu
from jax.sharding import PartitionSpec as P

MESH = pl.DeviceIdType.MESH
LANES = 128
SIDE = 256
TOTAL = SIDE * SIDE


def tables():
    k = np.arange(SIDE, dtype=np.float64)

    def cis(a, b, length):
        angle = 2.0 * np.pi * np.fmod(a[:, None] * b[None, :], length) / length
        return np.cos(angle), np.sin(angle)

    cos, sin = cis(k + 0.25, k, SIDE)
    rows = np.concatenate([cos, -sin], axis=0)
    back_rows = np.concatenate([cos.T, -sin.T], axis=1) / TOTAL
    twist = np.stack(cis(k + 0.25, k, TOTAL))
    cos, sin = cis(k, k, SIDE)
    columns = np.block([[cos, -sin], [sin, cos]])
    back_columns = np.block([[cos, sin], [-sin, cos]])
    bf16 = ml_dtypes.bfloat16
    return (
        rows.astype(bf16),
        columns.astype(bf16),
        back_columns.astype(bf16),
        back_rows.astype(bf16),
        twist.astype(np.float32),
    )


def kernel(
    n,
    proj_hbm, filt_hbm, taps_hbm, rows_hbm, cols_hbm, bcols_hbm, brows_hbm, twist_hbm,
    out,
    proj, filt, taps_ref, rows, cols, bcols, brows, twist, gate, stage,
    h_out, x_out, y_out, h_in, x_in, y_in, h_freq, back,
    load_sem, halo_send, halo_recv, h_send, h_recv, x_send, x_recv, y_send, y_recv, own_sem,
):
    f32, bf16 = jnp.float32, jnp.bfloat16
    me = lax.axis_index("ctx")
    width = filt.shape[1]
    tiles = width // LANES
    half = filt.shape[0] // 2

    loads = [
        pltpu.make_async_copy(filt_hbm, filt, load_sem.at[0]),
        pltpu.make_async_copy(proj_hbm, proj.at[:, :, pl.ds(LANES, width)], load_sem.at[1]),
        pltpu.make_async_copy(taps_hbm, taps_ref, load_sem.at[2]),
        pltpu.make_async_copy(rows_hbm, rows, load_sem.at[3]),
        pltpu.make_async_copy(twist_hbm, twist, load_sem.at[4]),
        pltpu.make_async_copy(cols_hbm, cols, load_sem.at[5]),
        pltpu.make_async_copy(bcols_hbm, bcols, load_sem.at[6]),
        pltpu.make_async_copy(brows_hbm, brows, load_sem.at[7]),
    ]
    for load in loads:
        load.start()

    barrier = pltpu.get_barrier_semaphore()

    def greet(step, carry):
        peer = lax.rem(me + step, n)
        pl.semaphore_signal(barrier, inc=1, device_id={"ctx": peer}, device_id_type=MESH)
        return carry

    lax.fori_loop(1, n, greet, 0)

    def block(ref, at):
        return ref.at[pl.ds(pl.multiple_of(at * 16, 16), 16)]

    def send_all(source, target, send_sem, recv_sem, own):
        def send(step, carry):
            peer = lax.rem(me + step, n)
            pltpu.make_async_remote_copy(
                src_ref=block(source, peer), dst_ref=block(target, me), send_sem=send_sem, recv_sem=recv_sem,
                device_id={"ctx": peer}, device_id_type=MESH,
            ).start()
            return carry

        lax.fori_loop(1, n, send, 0)
        pltpu.make_async_copy(block(source, me), block(target, me), own).start()

    def others(ref, send_sem, recv_sem):
        part = ref.at[pl.ds(0, 16 * (n - 1))]
        return pltpu.make_async_remote_copy(
            src_ref=part, dst_ref=part, send_sem=send_sem, recv_sem=recv_sem, device_id={"ctx": me}, device_id_type=MESH
        )

    def arrived(target, recv_sem, own):
        others(target, recv_sem, recv_sem).wait_recv()
        pltpu.make_async_copy(block(target, me), block(target, me), own).wait()

    def spread(value, group, tile_row, parity):
        stage[parity, pl.ds(group * 8 * 16 + tile_row, 8, stride=16), :] = value

    def gathered(target):
        target[:, 0:LANES] = stage[0].astype(bf16)
        target[:, LANES:SIDE] = stage[1].astype(bf16)

    loads[0].wait()

    def place_filter(j):
        def tile_pair(row, carry):
            for parity in range(2):
                at = pl.multiple_of((2 * row + parity) * LANES, LANES)
                value = filt[half * j : half * (j + 1), pl.ds(at, LANES)].astype(f32)
                for group in range(2):
                    spread(value[8 * group : 8 * group + 8], group, row, parity)
            return carry

        lax.fori_loop(0, tiles // 2, tile_pair, 0)
        gathered(h_out.at[j])

    place_filter(0)
    loads[1].wait()
    loads[2].wait()
    pl.semaphore_wait(barrier, n - 1)

    halo = pltpu.make_async_remote_copy(
        src_ref=proj.at[:, :, pl.ds(width, LANES)], dst_ref=proj.at[:, :, pl.ds(0, LANES)],
        send_sem=halo_send, recv_sem=halo_recv, device_id={"ctx": lax.rem(me + 1, n)}, device_id_type=MESH,
    )

    @pl.when(me < n - 1)
    def _():
        halo.start()

    @pl.when(me == 0)
    def _():
        proj[:, :, 0:LANES] = jnp.zeros((3, 2 * half, LANES), bf16)

    send_all(h_out.at[0], h_in.at[0], h_send.at[0], h_recv.at[0], own_sem.at[0])
    place_filter(1)
    send_all(h_out.at[1], h_in.at[1], h_send.at[1], h_recv.at[1], own_sem.at[1])

    diagonal = lax.broadcasted_iota(jnp.int32, (half, 2 * half), 0)
    along = lax.broadcasted_iota(jnp.int32, (half, 2 * half), 1)
    lane = lax.broadcasted_iota(jnp.int32, (half, LANES), 1)

    def tap(stream, lag, j):
        row = jnp.broadcast_to(taps_ref[stream, lag, :][None, :], (half, 2 * half))
        column = jnp.sum(jnp.where(along == diagonal + half * j, row, 0.0), axis=1, keepdims=True)
        return jnp.broadcast_to(column, (half, LANES))

    def tile_of(stream, at, j):
        start = pl.multiple_of(at * LANES, LANES)
        value = proj[stream, half * j : half * (j + 1), pl.ds(start, LANES)].astype(f32)
        return value, pltpu.roll(value, 1, 1), pltpu.roll(value, 2, 1)

    def short(taps, now, before):
        one = jnp.where(lane < 1, before[1], now[1])
        two = jnp.where(lane < 2, before[2], now[2])
        return taps[0] * now[0] + taps[1] * one + taps[2] * two

    def place_mixed(j):
        taps = [[tap(stream, lag, j) for lag in range(3)] for stream in (1, 2)]

        def one_tile(row, parity, now):
            before = [tile_of(stream, 2 * row + parity, j) for stream in (1, 2)]
            value = short(taps[0], now[0], before[0]) * short(taps[1], now[1], before[1])
            for group in range(2):
                spread(value[8 * group : 8 * group + 8], group, row, parity)
            return before

        def tile_pair(step, now):
            row = tiles // 2 - 1 - step
            return one_tile(row, 0, one_tile(row, 1, now))

        now = [tile_of(stream, tiles, j) for stream in (1, 2)]
        now = lax.fori_loop(0, tiles // 2 - 1, tile_pair, now)
        now = one_tile(0, 1, now)
        if j == 0:
            @pl.when(me > 0)
            def _():
                halo.wait_recv()
        one_tile(0, 0, now)
        gathered(x_out.at[j])
        send_all(x_out.at[j], x_in.at[j], x_send.at[j], x_recv.at[j], own_sem.at[2 + j])

    place_mixed(0)
    place_mixed(1)

    def place_gate(j):
        taps = [tap(0, lag, j) for lag in range(3)]

        def tile(at, before):
            now = tile_of(0, at + 1, j)
            gate[half * j : half * (j + 1), pl.ds(pl.multiple_of(at * LANES, LANES), LANES)] = short(taps, now, before)
            return now

        lax.fori_loop(0, tiles, tile, tile_of(0, 0, j))

    place_gate(0)
    place_gate(1)
    for load in loads[3:]:
        load.wait()

    def dot(a, b):
        return jnp.dot(a, b, preferred_element_type=f32)

    def forward(ref):
        part = dot(rows[...], ref[...])
        real, imag = part[:SIDE], part[SIDE:]
        cos, sin = twist[0], twist[1]
        turned = jnp.concatenate(
            [(real * cos + imag * sin).astype(bf16), (imag * cos - real * sin).astype(bf16)], axis=1
        )
        return dot(turned, cols[...])

    for j in range(2):
        arrived(h_in.at[j], h_recv.at[j], own_sem.at[j])
        h_freq[j] = forward(h_in.at[j])

    for j in range(2):
        arrived(x_in.at[j], x_recv.at[j], own_sem.at[2 + j])
        freq = forward(x_in.at[j])
        x_re, x_im = freq[:, :SIDE], freq[:, SIDE:]
        h_re, h_im = h_freq[j, :, :SIDE], h_freq[j, :, SIDE:]
        product = jnp.concatenate(
            [(x_re * h_re - x_im * h_im).astype(bf16), (x_re * h_im + x_im * h_re).astype(bf16)], axis=1
        )
        part = dot(product, bcols[...])
        real, imag = part[:, :SIDE], part[:, SIDE:]
        cos, sin = twist[0], twist[1]
        back[:SIDE] = (real * cos - imag * sin).astype(bf16)
        back[SIDE:] = (imag * cos + real * sin).astype(bf16)
        y_out[j] = dot(brows[...], back[...]).astype(bf16)
        send_all(y_out.at[j], y_in.at[j], y_send.at[j], y_recv.at[j], own_sem.at[4 + j])

    for j in range(2):
        arrived(y_in.at[j], y_recv.at[j], own_sem.at[4 + j])
        stage[0] = y_in[j, :, 0:LANES].astype(f32)
        stage[1] = y_in[j, :, LANES:SIDE].astype(f32)

        def tile_pair(row, carry):
            for parity in range(2):
                at = pl.multiple_of((2 * row + parity) * LANES, LANES)
                value = jnp.concatenate(
                    [stage[parity, pl.ds(group * 8 * 16 + row, 8, stride=16), :] for group in range(2)], axis=0
                )
                value = value * gate[half * j : half * (j + 1), pl.ds(at, LANES)]
                out[half * j : half * (j + 1), pl.ds(at, LANES)] = value.astype(bf16)
            return carry

        lax.fori_loop(0, tiles // 2, tile_pair, 0)

    @pl.when(me < n - 1)
    def _():
        halo.wait_send()

    for j in range(2):
        others(h_out.at[j], h_send.at[j], h_send.at[j]).wait_send()
        others(x_out.at[j], x_send.at[j], x_send.at[j]).wait_send()
        others(y_out.at[j], y_send.at[j], y_send.at[j]).wait_send()


def shards(n, projections, short_taps, long_filter):
    channels, width = long_filter.shape
    f32, bf16 = jnp.float32, jnp.bfloat16
    outside = pl.BlockSpec(memory_space=pltpu.HBM)
    inside = pl.BlockSpec(memory_space=pltpu.VMEM)
    square = pltpu.VMEM((2, SIDE, SIDE), bf16)
    pair = pltpu.SemaphoreType.DMA((2,))
    one = pltpu.SemaphoreType.DMA
    operands = [projections, long_filter, short_taps, *(jnp.asarray(t) for t in tables())]
    return pl.pallas_call(
        functools.partial(kernel, n),
        out_shape=jax.ShapeDtypeStruct((channels, width), bf16),
        in_specs=[outside] * 8,
        out_specs=inside,
        scratch_shapes=[
            pltpu.VMEM((3, channels, LANES + width), bf16),
            pltpu.VMEM((channels, width), bf16),
            pltpu.VMEM((3, 3, channels), f32),
            pltpu.VMEM((2 * SIDE, SIDE), bf16),
            pltpu.VMEM((2 * SIDE, 2 * SIDE), bf16),
            pltpu.VMEM((2 * SIDE, 2 * SIDE), bf16),
            pltpu.VMEM((SIDE, 2 * SIDE), bf16),
            pltpu.VMEM((2, SIDE, SIDE), f32),
            pltpu.VMEM((channels, width), f32),
            pltpu.VMEM((2, SIDE, LANES), f32),
            square, square, square, square, square, square,
            pltpu.VMEM((2, SIDE, 2 * SIDE), f32),
            pltpu.VMEM((2 * SIDE, SIDE), bf16),
            pltpu.SemaphoreType.DMA((8,)),
            one, one, pair, pair, pair, pair, pair, pair,
            pltpu.SemaphoreType.DMA((6,)),
        ],
        compiler_params=pltpu.CompilerParams(
            collective_id=0, has_side_effects=True, vmem_limit_bytes=32 * 1024 * 1024
        ),
        name="long_convolution",
    )(*(pltpu.with_memory_space_constraint(x, pltpu.HBM) for x in operands))


def solution(mesh):
    in_specs = (P(None, "chan", "ctx"), P(None, None, "chan"), P("chan", "ctx"))
    return jax.shard_map(
        functools.partial(shards, mesh.shape["ctx"]),
        mesh=mesh, in_specs=in_specs, out_specs=P("chan", "ctx"), check_vma=False,
    )
```

```python
import functools
import math

import jax
import jax.numpy as jnp
import ml_dtypes
import numpy as np
from jax import lax
from jax.experimental import pallas as pl
from jax.experimental.pallas import tpu as pltpu
from jax.sharding import PartitionSpec as P

MESH = pl.DeviceIdType.MESH
LANES = 128
SIDE = 256
TOTAL = SIDE * SIDE


def tables():
    k = np.arange(SIDE, dtype=np.float64)

    def cis(a, b, length):
        angle = 2.0 * np.pi * np.fmod(a[:, None] * b[None, :], length) / length
        return np.cos(angle), np.sin(angle)

    cos, sin = cis(k + 0.25, k, SIDE)
    rows = np.concatenate([cos, -sin], axis=0)
    back_rows = np.concatenate([cos.T, -sin.T], axis=1) / TOTAL
    twist = np.stack(cis(k + 0.25, k, TOTAL))
    cos, sin = cis(k, k, SIDE)
    columns = np.block([[cos, -sin], [sin, cos]])
    back_columns = np.block([[cos, sin], [-sin, cos]])
    bf16 = ml_dtypes.bfloat16
    return (
        rows.astype(bf16),
        columns.astype(bf16),
        back_columns.astype(bf16),
        back_rows.astype(bf16),
        twist.astype(np.float32),
    )


def peers_of(me, n):
    side = math.isqrt(n)

    def hops(step):
        return sum(min(s, side - s) for s in step)

    steps = [(a, b) for a in range(side) for b in range(side) if a or b]
    row, column = me // side, lax.rem(me, side)
    return [
        lax.rem(row + a, side) * side + lax.rem(column + b, side)
        for a, b in sorted(steps, key=hops, reverse=True)
    ]


def kernel(
    n,
    proj_hbm, filt_hbm, taps_hbm, rows_hbm, cols_hbm, bcols_hbm, brows_hbm, twist_hbm,
    out,
    proj, filt, taps_ref, rows, cols, bcols, brows, twist, gate, stage, q_halo, head,
    h_out, x_out, y_out, h_in, x_in, y_in, e_out, e_in, h_freq, back,
    load_sem, halo_send, halo_recv, h_send, h_recv, x_send, x_recv, y_send, y_recv, e_send, e_recv, own_sem,
):
    f32, bf16 = jnp.float32, jnp.bfloat16
    me = lax.axis_index("ctx")
    peers = peers_of(me, n)
    width = filt.shape[1]
    tiles = width // LANES
    half = filt.shape[0] // 2

    barrier = pltpu.get_barrier_semaphore()
    for peer in peers:
        pl.semaphore_signal(barrier, inc=1, device_id={"ctx": peer}, device_id_type=MESH)
    loads = [
        pltpu.make_async_copy(source, target, load_sem.at[at])
        for at, (source, target) in enumerate([
            (filt_hbm, filt), (taps_hbm, taps_ref), (proj_hbm.at[1], proj.at[1]), (proj_hbm.at[2], proj.at[2]),
            (proj_hbm.at[0], proj.at[0]), (rows_hbm, rows), (twist_hbm, twist), (cols_hbm, cols),
            (bcols_hbm, bcols), (brows_hbm, brows),
        ])
    ]
    for load in loads:
        load.start()

    def block(ref, at):
        return ref.at[pl.ds(pl.multiple_of(at * 16, 16), 16)]

    def remote(source, target, send_sem, recv_sem, peer):
        return pltpu.make_async_remote_copy(
            src_ref=source, dst_ref=target, send_sem=send_sem, recv_sem=recv_sem,
            device_id={"ctx": peer}, device_id_type=MESH,
        )

    def send_all(source, target, send_sem, recv_sem, own, part=block):
        for peer in peers:
            remote(part(source, peer), part(target, me), send_sem, recv_sem, peer).start()
        pltpu.make_async_copy(part(source, me), part(target, me), own).start()

    def others(ref, send_sem, recv_sem):
        size = ref.shape[0] // n * (n - 1)
        return remote(ref.at[pl.ds(0, size)], ref.at[pl.ds(0, size)], send_sem, recv_sem, me)

    def arrived(target, recv_sem, own, part=block):
        others(target, recv_sem, recv_sem).wait_recv()
        pltpu.make_async_copy(part(target, me), part(target, me), own).wait()

    def spread(value, group, tile_row, parity):
        stage[parity, pl.ds(group * 8 * 16 + tile_row, 8, stride=16), :] = value

    def gathered(target):
        target[:, 0:LANES] = stage[0].astype(bf16)
        target[:, LANES:SIDE] = stage[1].astype(bf16)

    def place_filter(j):
        def tile_pair(row, carry):
            for parity in range(2):
                at = pl.multiple_of((2 * row + parity) * LANES, LANES)
                value = filt[half * j : half * (j + 1), pl.ds(at, LANES)].astype(f32)
                for group in range(2):
                    spread(value[8 * group : 8 * group + 8], group, row, parity)
            return carry

        lax.fori_loop(0, tiles // 2, tile_pair, 0, unroll=True)
        gathered(h_out.at[j])

    diagonal = lax.broadcasted_iota(jnp.int32, (half, 2 * half), 0)
    along = lax.broadcasted_iota(jnp.int32, (half, 2 * half), 1)
    lane = lax.broadcasted_iota(jnp.int32, (half, LANES), 1)
    lag_range, zero = range(3), jnp.zeros((half, LANES), f32)

    def tap(stream, lag, j):
        row = jnp.broadcast_to(taps_ref[stream, lag, :][None, :], (half, 2 * half))
        column = jnp.sum(jnp.where(along == diagonal + half * j, row, 0.0), axis=1, keepdims=True)
        return jnp.broadcast_to(column, (half, LANES))

    def own_tap(stream, lag, j):
        row = jnp.broadcast_to(taps_ref[stream, lag, :][None, :], (half, 2 * half))
        column = jnp.sum(jnp.where(along == me + half * j, row, 0.0), axis=1, keepdims=True)
        return jnp.broadcast_to(column, (half, LANES))

    def rolled(value):
        return value, pltpu.roll(value, 1, 1), pltpu.roll(value, 2, 1)

    def tile_of(stream, at, j):
        start = pl.multiple_of(at * LANES, LANES)
        return rolled(proj[stream, half * j : half * (j + 1), pl.ds(start, LANES)].astype(f32))

    def short(taps, now, before):
        one = jnp.where(lane < 1, before[1], now[1])
        two = jnp.where(lane < 2, before[2], now[2])
        return taps[0] * now[0] + taps[1] * one + taps[2] * two

    def place_mixed(j):
        taps = [[tap(stream, lag, j) for lag in lag_range] for stream in (1, 2)]

        def one_tile(row, parity, now, before):
            value = short(taps[0], now[0], before[0]) * short(taps[1], now[1], before[1])
            for group in range(2):
                spread(value[8 * group : 8 * group + 8], group, row, parity)

        def tile_pair(row, before):
            for parity in range(2):
                now = [tile_of(stream, 2 * row + parity, j) for stream in (1, 2)]
                one_tile(row, parity, now, before)
                before = now
            return before

        lax.fori_loop(0, tiles // 2, tile_pair, [(zero, zero, zero)] * 2, unroll=True)
        gathered(x_out.at[j])

    def place_edges():
        edges = zero
        for g in range(4):
            channels = slice(half * (g // 2), half * (g // 2) + half)
            first = proj[1 + g % 2, channels, 0:LANES].astype(f32)
            last = proj[1 + g % 2, channels, width - LANES : width].astype(f32)
            edges = jnp.where((lane >= 32 * g) & (lane < 32 * g + 16), pltpu.roll(first, 32 * g, 1) if g else first, edges)
            edges = jnp.where(
                (lane >= 32 * g + 16) & (lane < 32 * g + 32), pltpu.roll(last, 32 * (g + 1), 1) if g < 3 else last, edges
            )
        e_out[...] = edges[:, None, :]

    def place_heads():
        edges = e_in[...].reshape(n, LANES)
        earlier = jnp.where(lax.broadcasted_iota(jnp.int32, (n, LANES), 0) < 1, 0.0, pltpu.roll(edges, 1, 0))
        for j in range(2):
            product = None
            for stream in (1, 2):
                g = 2 * j + stream - 1
                now = pltpu.roll(edges, LANES - 32 * g, 1) if g else edges
                one = jnp.where(lane < 1, pltpu.roll(earlier, (2 * LANES - 32 * g - 31) % LANES, 1), pltpu.roll(now, 1, 1))
                two = pltpu.roll(earlier, (2 * LANES - 32 * g - 30) % LANES, 1)
                taps = [own_tap(stream, lag, j) for lag in lag_range]
                value = taps[0] * now + taps[1] * one + taps[2] * two
                product = value if product is None else product * value
            for group in range(2):
                head[j, pl.ds(group * 8 * 16, 8, stride=16), :] = product[8 * group : 8 * group + 8]

    def mixed_of(j):
        at_row = lax.broadcasted_iota(jnp.int32, (SIDE, LANES), 0)
        at_lane = lax.broadcasted_iota(jnp.int32, (SIDE, LANES), 1)
        is_head = (lax.rem(at_row, 16) == 0) & (at_lane < 2)
        even = jnp.where(is_head, head[j], x_in[j, :, 0:LANES].astype(f32)).astype(bf16)
        return jnp.concatenate([even, x_in[j, :, LANES:SIDE]], axis=1)

    def place_gate(j):
        taps = [tap(0, lag, j) for lag in lag_range]

        def tile(at, before):
            now = tile_of(0, at, j)
            gate[half * j : half * (j + 1), pl.ds(pl.multiple_of(at * LANES, LANES), LANES)] = short(taps, now, before)
            return now

        before = rolled(jnp.where(me > 0, q_halo[half * j : half * (j + 1), :].astype(f32), 0.0))
        lax.fori_loop(0, tiles, tile, before, unroll=True)

    def dot(a, b):
        return jnp.dot(a, b, preferred_element_type=f32)

    def forward(value):
        part = dot(rows[...], value)
        real, imag = part[:SIDE], part[SIDE:]
        cos, sin = twist[0], twist[1]
        turned = jnp.concatenate(
            [(real * cos + imag * sin).astype(bf16), (imag * cos - real * sin).astype(bf16)], axis=1
        )
        return dot(turned, cols[...])

    def whole(ref, at):
        return ref.at[pl.ds(at, 1)]

    loads[0].wait()
    place_filter(0)
    place_filter(1)
    for load in loads[1:4]:
        load.wait()
    place_edges()
    pl.semaphore_wait(barrier, n - 1)
    send_all(h_out.at[0], h_in.at[0], h_send.at[0], h_recv.at[0], own_sem.at[0])
    send_all(e_out, e_in, e_send, e_recv, own_sem.at[6], part=whole)
    place_mixed(0)
    send_all(x_out.at[0], x_in.at[0], x_send.at[0], x_recv.at[0], own_sem.at[2])
    send_all(h_out.at[1], h_in.at[1], h_send.at[1], h_recv.at[1], own_sem.at[1])
    place_mixed(1)
    send_all(x_out.at[1], x_in.at[1], x_send.at[1], x_recv.at[1], own_sem.at[3])
    loads[4].wait()
    last = proj.at[0, :, pl.ds(width - LANES, LANES)]
    halo = remote(last, q_halo, halo_send, halo_recv, lax.rem(me + 1, n))
    halo.start()
    for load in loads[5:]:
        load.wait()

    for j in range(2):
        arrived(h_in.at[j], h_recv.at[j], own_sem.at[j])
        h_freq[...] = forward(h_in[j])
        if j == 0:
            arrived(e_in, e_recv, own_sem.at[6], part=whole)
            place_heads()
        arrived(x_in.at[j], x_recv.at[j], own_sem.at[2 + j])
        freq = forward(mixed_of(j))
        x_re, x_im = freq[:, :SIDE], freq[:, SIDE:]
        h_re, h_im = h_freq[:, :SIDE], h_freq[:, SIDE:]
        product = jnp.concatenate(
            [(x_re * h_re - x_im * h_im).astype(bf16), (x_re * h_im + x_im * h_re).astype(bf16)], axis=1
        )
        part = dot(product, bcols[...])
        real, imag = part[:, :SIDE], part[:, SIDE:]
        cos, sin = twist[0], twist[1]
        back[:SIDE] = (real * cos - imag * sin).astype(bf16)
        back[SIDE:] = (imag * cos + real * sin).astype(bf16)
        y_out[j] = dot(brows[...], back[...]).astype(bf16)
        send_all(y_out.at[j], y_in.at[j], y_send.at[j], y_recv.at[j], own_sem.at[4 + j])

    halo.wait_recv()
    place_gate(0)
    place_gate(1)

    for j in range(2):
        arrived(y_in.at[j], y_recv.at[j], own_sem.at[4 + j])
        stage[0] = y_in[j, :, 0:LANES].astype(f32)
        stage[1] = y_in[j, :, LANES:SIDE].astype(f32)

        def tile_pair(row, carry):
            for parity in range(2):
                at = pl.multiple_of((2 * row + parity) * LANES, LANES)
                value = jnp.concatenate(
                    [stage[parity, pl.ds(group * 8 * 16 + row, 8, stride=16), :] for group in range(2)], axis=0
                )
                value = value * gate[half * j : half * (j + 1), pl.ds(at, LANES)]
                out[half * j : half * (j + 1), pl.ds(at, LANES)] = value.astype(bf16)
            return carry

        lax.fori_loop(0, tiles // 2, tile_pair, 0, unroll=True)

    halo.wait_send()
    others(e_out, e_send, e_send).wait_send()
    for j in range(2):
        others(h_out.at[j], h_send.at[j], h_send.at[j]).wait_send()
        others(x_out.at[j], x_send.at[j], x_send.at[j]).wait_send()
        others(y_out.at[j], y_send.at[j], y_send.at[j]).wait_send()


def shards(n, projections, short_taps, long_filter):
    channels, width = long_filter.shape
    f32, bf16 = jnp.float32, jnp.bfloat16
    outside = pl.BlockSpec(memory_space=pltpu.HBM)
    inside = pl.BlockSpec(memory_space=pltpu.VMEM)
    square = pltpu.VMEM((2, SIDE, SIDE), bf16)
    edges = pltpu.VMEM((n, 1, LANES), f32)
    pair = pltpu.SemaphoreType.DMA((2,))
    one = pltpu.SemaphoreType.DMA
    operands = [projections, long_filter, short_taps, *(jnp.asarray(t) for t in tables())]
    return pl.pallas_call(
        functools.partial(kernel, n),
        out_shape=jax.ShapeDtypeStruct((channels, width), bf16),
        in_specs=[outside] * 8,
        out_specs=inside,
        scratch_shapes=[
            pltpu.VMEM((3, channels, width), bf16),
            pltpu.VMEM((channels, width), bf16),
            pltpu.VMEM((3, 3, channels), f32),
            pltpu.VMEM((2 * SIDE, SIDE), bf16),
            pltpu.VMEM((2 * SIDE, 2 * SIDE), bf16),
            pltpu.VMEM((2 * SIDE, 2 * SIDE), bf16),
            pltpu.VMEM((SIDE, 2 * SIDE), bf16),
            pltpu.VMEM((2, SIDE, SIDE), f32),
            pltpu.VMEM((channels, width), f32),
            pltpu.VMEM((2, SIDE, LANES), f32),
            pltpu.VMEM((channels, LANES), bf16),
            pltpu.VMEM((2, SIDE, LANES), f32),
            square, square, square, square, square, square,
            edges, edges,
            pltpu.VMEM((SIDE, 2 * SIDE), f32),
            pltpu.VMEM((2 * SIDE, SIDE), bf16),
            pltpu.SemaphoreType.DMA((10,)),
            one, one, pair, pair, pair, pair, pair, pair, one, one,
            pltpu.SemaphoreType.DMA((7,)),
        ],
        compiler_params=pltpu.CompilerParams(
            collective_id=0, has_side_effects=True, vmem_limit_bytes=32 * 1024 * 1024
        ),
        name="long_convolution",
    )(*(pltpu.with_memory_space_constraint(x, pltpu.HBM) for x in operands))


def solution(mesh):
    in_specs = (P(None, "chan", "ctx"), P(None, None, "chan"), P("chan", "ctx"))
    return jax.shard_map(
        functools.partial(shards, mesh.shape["ctx"]),
        mesh=mesh, in_specs=in_specs, out_specs=P("chan", "ctx"), check_vma=False,
    )
```

```python
import functools
import math

import jax
import jax.numpy as jnp
import ml_dtypes
import numpy as np
from jax import lax
from jax.experimental import pallas as pl
from jax.experimental.pallas import tpu as pltpu
from jax.sharding import PartitionSpec as P

MESH = pl.DeviceIdType.MESH
LANES = 128
SIDE = 256
TOTAL = SIDE * SIDE


def tables():
    k = np.arange(SIDE, dtype=np.float64)

    def cis(a, b, length):
        angle = 2.0 * np.pi * np.fmod(a[:, None] * b[None, :], length) / length
        return np.cos(angle), np.sin(angle)

    cos, sin = cis(k + 0.25, k, SIDE)
    rows = np.concatenate([cos, -sin], axis=0)
    back_rows = np.concatenate([cos.T, -sin.T], axis=1) / TOTAL
    twist = np.stack(cis(k + 0.25, k, TOTAL))
    cos, sin = cis(k, k, SIDE)
    columns = np.block([[cos, -sin], [sin, cos]])
    back_columns = np.block([[cos, sin], [-sin, cos]])
    bf16 = ml_dtypes.bfloat16
    return (
        rows.astype(bf16),
        columns.astype(bf16),
        back_columns.astype(bf16),
        back_rows.astype(bf16),
        twist.astype(np.float32),
    )


def steps_of(n):
    side = math.isqrt(n)
    steps = [(a, b) for a in range(side) for b in range(side) if a or b]
    return sorted(steps, key=lambda step: -sum(min(s, side - s) for s in step))


def kernel(
    n,
    proj_hbm, filt_hbm, taps_hbm, rows_hbm, cols_hbm, bcols_hbm, brows_hbm, twist_hbm,
    out,
    proj, filt, taps_ref, rows, cols, bcols, brows, twist, gate, stage, q_halo, head,
    h_out, x_out, y_out, h_in, x_in, y_in, e_out, e_in, h_freq,
    load_sem, halo_send, halo_recv, h_send, h_recv, x_send, x_recv, y_send, y_recv, e_send, e_recv, own_sem, column_in,
):
    f32, bf16 = jnp.float32, jnp.bfloat16
    me = lax.axis_index("ctx")
    side = math.isqrt(n)
    my_row, my_column = me // side, lax.rem(me, side)

    def device(step):
        return lax.rem(my_row + step[0], side) * side + lax.rem(my_column + step[1], side)

    steps = steps_of(n)
    mates = [step for step in steps if not (step[0] and step[1])]
    width = filt.shape[1]
    tiles = width // LANES
    half = filt.shape[0] // 2

    barrier = pltpu.get_barrier_semaphore()
    for step in mates:
        pl.semaphore_signal(barrier, inc=1, device_id={"ctx": device(step)}, device_id_type=MESH)
    loads = [
        pltpu.make_async_copy(source, target, load_sem.at[at])
        for at, (source, target) in enumerate([
            (filt_hbm, filt), (taps_hbm, taps_ref), (proj_hbm.at[1], proj.at[1]), (proj_hbm.at[2], proj.at[2]),
            (proj_hbm.at[0], proj.at[0]), (rows_hbm, rows), (twist_hbm, twist), (cols_hbm, cols),
            (bcols_hbm, bcols), (brows_hbm, brows),
        ])
    ]
    for load in loads:
        load.start()

    def block(ref, at):
        return ref.at[pl.ds(at, 1)]

    def remote(source, target, send_sem, recv_sem, peer):
        return pltpu.make_async_remote_copy(
            src_ref=source, dst_ref=target, send_sem=send_sem, recv_sem=recv_sem,
            device_id={"ctx": peer}, device_id_type=MESH,
        )

    def send(source, target, send_sem, recv_sem, chosen, part=block):
        for step in chosen:
            peer = device(step)
            remote(part(source, peer), part(target, me), send_sem, recv_sem, peer).start()

    def keep(source, target, own, part=block):
        pltpu.make_async_copy(part(source, me), part(target, me), own).start()

    def others(ref, send_sem, recv_sem):
        size = ref.shape[0] // n * (n - 1)
        return remote(ref.at[pl.ds(0, size)], ref.at[pl.ds(0, size)], send_sem, recv_sem, me)

    def arrived(target, recv_sem, own, part=block):
        others(target, recv_sem, recv_sem).wait_recv()
        pltpu.make_async_copy(part(target, me), part(target, me), own).wait()

    def spread(value, group, tile_row, parity):
        stage[parity, pl.ds(group * 8 * 16 + tile_row, 8, stride=16), :] = value

    def gathered(target):
        for parity in range(2):
            target[:, :, LANES * parity : LANES * (parity + 1)] = stage[parity].astype(bf16).reshape(n, 16, LANES)

    def place_filter(j):
        def tile_pair(row, carry):
            for parity in range(2):
                at = pl.multiple_of((2 * row + parity) * LANES, LANES)
                value = filt[half * j : half * (j + 1), pl.ds(at, LANES)].astype(f32)
                for group in range(2):
                    spread(value[8 * group : 8 * group + 8], group, row, parity)
            return carry

        lax.fori_loop(0, tiles // 2, tile_pair, 0, unroll=True)
        gathered(h_out.at[j])

    diagonal = lax.broadcasted_iota(jnp.int32, (half, 2 * half), 0)
    along = lax.broadcasted_iota(jnp.int32, (half, 2 * half), 1)
    lane = lax.broadcasted_iota(jnp.int32, (half, LANES), 1)
    lag_range, zero = range(3), jnp.zeros((half, LANES), f32)

    def tap(stream, lag, j):
        row = jnp.broadcast_to(taps_ref[stream, lag, :][None, :], (half, 2 * half))
        column = jnp.sum(jnp.where(along == diagonal + half * j, row, 0.0), axis=1, keepdims=True)
        return jnp.broadcast_to(column, (half, LANES))

    def own_tap(stream, lag, j):
        row = jnp.broadcast_to(taps_ref[stream, lag, :][None, :], (half, 2 * half))
        column = jnp.sum(jnp.where(along == me + half * j, row, 0.0), axis=1, keepdims=True)
        return jnp.broadcast_to(column, (half, LANES))

    def rolled(value):
        return value, pltpu.roll(value, 1, 1), pltpu.roll(value, 2, 1)

    def tile_of(stream, at, j):
        start = pl.multiple_of(at * LANES, LANES)
        return rolled(proj[stream, half * j : half * (j + 1), pl.ds(start, LANES)].astype(f32))

    def short(taps, now, before):
        one = jnp.where(lane < 1, before[1], now[1])
        two = jnp.where(lane < 2, before[2], now[2])
        return taps[0] * now[0] + taps[1] * one + taps[2] * two

    def place_mixed(j):
        taps = [[tap(stream, lag, j) for lag in lag_range] for stream in (1, 2)]

        def one_tile(row, parity, now, before):
            value = short(taps[0], now[0], before[0]) * short(taps[1], now[1], before[1])
            for group in range(2):
                spread(value[8 * group : 8 * group + 8], group, row, parity)

        def tile_pair(row, before):
            for parity in range(2):
                now = [tile_of(stream, 2 * row + parity, j) for stream in (1, 2)]
                one_tile(row, parity, now, before)
                before = now
            return before

        lax.fori_loop(0, tiles // 2, tile_pair, [(zero, zero, zero)] * 2, unroll=True)
        gathered(x_out.at[j])

    def place_edges():
        edges = zero
        for g in range(4):
            channels = slice(half * (g // 2), half * (g // 2) + half)
            first = proj[1 + g % 2, channels, 0:LANES].astype(f32)
            last = proj[1 + g % 2, channels, width - LANES : width].astype(f32)
            edges = jnp.where((lane >= 32 * g) & (lane < 32 * g + 16), pltpu.roll(first, 32 * g, 1) if g else first, edges)
            edges = jnp.where(
                (lane >= 32 * g + 16) & (lane < 32 * g + 32), pltpu.roll(last, 32 * (g + 1), 1) if g < 3 else last, edges
            )
        e_out[...] = edges[:, None, :]

    def place_heads():
        edges = e_in[...].reshape(n, LANES)
        earlier = jnp.where(lax.broadcasted_iota(jnp.int32, (n, LANES), 0) < 1, 0.0, pltpu.roll(edges, 1, 0))
        for j in range(2):
            product = None
            for stream in (1, 2):
                g = 2 * j + stream - 1
                now = pltpu.roll(edges, LANES - 32 * g, 1) if g else edges
                one = jnp.where(lane < 1, pltpu.roll(earlier, (2 * LANES - 32 * g - 31) % LANES, 1), pltpu.roll(now, 1, 1))
                two = pltpu.roll(earlier, (2 * LANES - 32 * g - 30) % LANES, 1)
                taps = [own_tap(stream, lag, j) for lag in lag_range]
                value = taps[0] * now + taps[1] * one + taps[2] * two
                product = value if product is None else product * value
            for group in range(2):
                head[j, pl.ds(group * 8 * 16, 8, stride=16), :] = product[8 * group : 8 * group + 8]

    def mixed_of(j):
        at_row = lax.broadcasted_iota(jnp.int32, (SIDE, LANES), 0)
        at_lane = lax.broadcasted_iota(jnp.int32, (SIDE, LANES), 1)
        is_head = (lax.rem(at_row, 16) == 0) & (at_lane < 2)
        value = x_in[j].reshape(SIDE, SIDE)
        even = jnp.where(is_head, head[j], value[:, 0:LANES].astype(f32)).astype(bf16)
        return jnp.concatenate([even, value[:, LANES:SIDE]], axis=1)

    def place_gate(j):
        taps = [tap(0, lag, j) for lag in lag_range]

        def tile(at, before):
            now = tile_of(0, at, j)
            gate[half * j : half * (j + 1), pl.ds(pl.multiple_of(at * LANES, LANES), LANES)] = short(taps, now, before)
            return now

        before = rolled(jnp.where(me > 0, q_halo[half * j : half * (j + 1), :].astype(f32), 0.0))
        lax.fori_loop(0, tiles, tile, before, unroll=True)

    def dot(a, b):
        return jnp.dot(a, b, preferred_element_type=f32)

    def forward(values):
        part = dot(rows[...], jnp.concatenate(values, axis=1))
        cos, sin = twist[0], twist[1]
        turned = []
        for at in range(len(values)):
            columns = slice(SIDE * at, SIDE * (at + 1))
            real, imag = part[:SIDE, columns], part[SIDE:, columns]
            turned.append(
                jnp.concatenate([(real * cos + imag * sin).astype(bf16), (imag * cos - real * sin).astype(bf16)], axis=1)
            )
        return dot(jnp.concatenate(turned, axis=0), cols[...])

    def convolved(x, h):
        x_re, x_im, h_re, h_im = x[:, :SIDE], x[:, SIDE:], h[:, :SIDE], h[:, SIDE:]
        product = jnp.concatenate(
            [(x_re * h_re - x_im * h_im).astype(bf16), (x_re * h_im + x_im * h_re).astype(bf16)], axis=1
        )
        part = dot(product, bcols[...])
        real, imag = part[:, :SIDE], part[:, SIDE:]
        cos, sin = twist[0], twist[1]
        turned = jnp.concatenate(
            [(real * cos - imag * sin).astype(bf16), (imag * cos + real * sin).astype(bf16)], axis=0
        )
        return dot(brows[...], turned).astype(bf16).reshape(n, 16, SIDE)

    def filter_of(j):
        return h_in[j].reshape(SIDE, SIDE)

    loads[0].wait()
    place_filter(0)
    place_filter(1)
    for load in loads[1:4]:
        load.wait()
    place_edges()
    pl.semaphore_wait(barrier, len(mates))
    for step in mates:
        if step[0]:
            pl.semaphore_signal(
                column_in.at[my_row], inc=1, device_id={"ctx": device(step)}, device_id_type=MESH
            )
    send(h_out.at[0], h_in.at[0], h_send.at[0], h_recv.at[0], mates)
    place_mixed(0)
    send(e_out, e_in, e_send, e_recv, mates)
    send(x_out.at[0], x_in.at[0], x_send.at[0], x_recv.at[0], mates)
    send(h_out.at[1], h_in.at[1], h_send.at[1], h_recv.at[1], mates)
    place_mixed(1)
    send(x_out.at[1], x_in.at[1], x_send.at[1], x_recv.at[1], mates)
    keep(e_out, e_in, own_sem.at[6])
    for j in range(2):
        keep(h_out.at[j], h_in.at[j], own_sem.at[j])
        keep(x_out.at[j], x_in.at[j], own_sem.at[2 + j])
    for far in (1, side - 1, 2):
        pl.semaphore_wait(column_in.at[lax.rem(my_row + far, side)], 1)
        chosen = [step for step in steps if step[0] == far and step[1]]
        send(h_out.at[0], h_in.at[0], h_send.at[0], h_recv.at[0], chosen)
        send(e_out, e_in, e_send, e_recv, chosen)
        send(x_out.at[0], x_in.at[0], x_send.at[0], x_recv.at[0], chosen)
    chosen = [step for step in steps if step[0] and step[1]]
    send(h_out.at[1], h_in.at[1], h_send.at[1], h_recv.at[1], chosen)
    send(x_out.at[1], x_in.at[1], x_send.at[1], x_recv.at[1], chosen)
    loads[4].wait()
    last = proj.at[0, :, pl.ds(width - LANES, LANES)]
    halo = remote(last, q_halo, halo_send, halo_recv, lax.rem(me + 1, n))
    halo.start()
    for load in loads[5:]:
        load.wait()

    arrived(h_in.at[0], h_recv.at[0], own_sem.at[0])
    h_freq[...] = forward([filter_of(0)])
    arrived(e_in, e_recv, own_sem.at[6])
    place_heads()
    arrived(x_in.at[0], x_recv.at[0], own_sem.at[2])
    y_out[0] = convolved(forward([mixed_of(0)]), h_freq[...])
    send(y_out.at[0], y_in.at[0], y_send.at[0], y_recv.at[0], steps)
    keep(y_out.at[0], y_in.at[0], own_sem.at[4])
    arrived(h_in.at[1], h_recv.at[1], own_sem.at[1])
    arrived(x_in.at[1], x_recv.at[1], own_sem.at[3])
    both = forward([mixed_of(1), filter_of(1)])
    y_out[1] = convolved(both[:SIDE], both[SIDE:])
    send(y_out.at[1], y_in.at[1], y_send.at[1], y_recv.at[1], steps)
    keep(y_out.at[1], y_in.at[1], own_sem.at[5])

    halo.wait_recv()
    place_gate(0)
    place_gate(1)

    for j in range(2):
        arrived(y_in.at[j], y_recv.at[j], own_sem.at[4 + j])
        stage[0] = y_in[j, :, :, 0:LANES].astype(f32).reshape(SIDE, LANES)
        stage[1] = y_in[j, :, :, LANES:SIDE].astype(f32).reshape(SIDE, LANES)

        def tile_pair(row, carry):
            for parity in range(2):
                at = pl.multiple_of((2 * row + parity) * LANES, LANES)
                value = jnp.concatenate(
                    [stage[parity, pl.ds(group * 8 * 16 + row, 8, stride=16), :] for group in range(2)], axis=0
                )
                value = value * gate[half * j : half * (j + 1), pl.ds(at, LANES)]
                out[half * j : half * (j + 1), pl.ds(at, LANES)] = value.astype(bf16)
            return carry

        lax.fori_loop(0, tiles // 2, tile_pair, 0, unroll=True)

    halo.wait_send()
    others(e_out, e_send, e_send).wait_send()
    for j in range(2):
        others(h_out.at[j], h_send.at[j], h_send.at[j]).wait_send()
        others(x_out.at[j], x_send.at[j], x_send.at[j]).wait_send()
        others(y_out.at[j], y_send.at[j], y_send.at[j]).wait_send()


def shards(n, projections, short_taps, long_filter):
    channels, width = long_filter.shape
    f32, bf16 = jnp.float32, jnp.bfloat16
    outside = pl.BlockSpec(memory_space=pltpu.HBM)
    inside = pl.BlockSpec(memory_space=pltpu.VMEM)
    halves = pltpu.VMEM((2, n, SIDE // n, SIDE), bf16)
    edges = pltpu.VMEM((n, 1, LANES), f32)
    pair = pltpu.SemaphoreType.DMA((2,))
    one = pltpu.SemaphoreType.DMA
    operands = [projections, long_filter, short_taps, *(jnp.asarray(t) for t in tables())]
    return pl.pallas_call(
        functools.partial(kernel, n),
        out_shape=jax.ShapeDtypeStruct((channels, width), bf16),
        in_specs=[outside] * 8,
        out_specs=inside,
        scratch_shapes=[
            pltpu.VMEM((3, channels, width), bf16),
            pltpu.VMEM((channels, width), bf16),
            pltpu.VMEM((3, 3, channels), f32),
            pltpu.VMEM((2 * SIDE, SIDE), bf16),
            pltpu.VMEM((2 * SIDE, 2 * SIDE), bf16),
            pltpu.VMEM((2 * SIDE, 2 * SIDE), bf16),
            pltpu.VMEM((SIDE, 2 * SIDE), bf16),
            pltpu.VMEM((2, SIDE, SIDE), f32),
            pltpu.VMEM((channels, width), f32),
            pltpu.VMEM((2, SIDE, LANES), f32),
            pltpu.VMEM((channels, LANES), bf16),
            pltpu.VMEM((2, SIDE, LANES), f32),
            halves, halves, halves, halves, halves, halves, edges, edges,
            pltpu.VMEM((SIDE, 2 * SIDE), f32),
            pltpu.SemaphoreType.DMA((10,)),
            one, one, pair, pair, pair, pair, pair, pair, one, one,
            pltpu.SemaphoreType.DMA((7,)),
            pltpu.SemaphoreType.REGULAR((math.isqrt(n),)),
        ],
        compiler_params=pltpu.CompilerParams(
            collective_id=0, has_side_effects=True, vmem_limit_bytes=32 * 1024 * 1024
        ),
        name="long_convolution",
    )(*(pltpu.with_memory_space_constraint(x, pltpu.HBM) for x in operands))


def solution(mesh):
    in_specs = (P(None, "chan", "ctx"), P(None, None, "chan"), P("chan", "ctx"))
    return jax.shard_map(
        functools.partial(shards, mesh.shape["ctx"]),
        mesh=mesh, in_specs=in_specs, out_specs=P("chan", "ctx"), check_vma=False,
    )
```

```python
import functools
import math

import jax
import jax.numpy as jnp
import ml_dtypes
import numpy as np
from jax import lax
from jax.experimental import pallas as pl
from jax.experimental.pallas import tpu as pltpu
from jax.sharding import PartitionSpec as P

MESH = pl.DeviceIdType.MESH
LANES = 128
SIDE = 256
TOTAL = SIDE * SIDE
PARTS = 16


def tables():
    k = np.arange(SIDE, dtype=np.float64)

    def cis(a, b, length):
        angle = 2.0 * np.pi * np.fmod(a[:, None] * b[None, :], length) / length
        return np.cos(angle), np.sin(angle)

    cos, sin = cis(k + 0.25, k, SIDE)
    rows = np.concatenate([cos, -sin], axis=1)
    back_rows = np.concatenate([cos.T, -sin.T], axis=1) / TOTAL
    twist = np.stack(cis(k + 0.25, k, TOTAL))
    cos, sin = cis(k, k, SIDE)
    columns = np.block([[cos, -sin], [sin, cos]])
    back_columns = np.block([[cos, sin], [-sin, cos]])
    dft = np.concatenate([rows, back_rows, columns, back_columns], axis=0)

    steps = SIDE // PARTS
    few = np.arange(steps, dtype=np.float64)
    cos, sin = cis(few + 0.25, few, steps)
    every = np.eye(PARTS)
    rows = np.concatenate([np.kron(every, cos), np.kron(every, -sin)], axis=1)
    back_rows = np.concatenate([np.kron(every, cos.T), np.kron(every, -sin.T)], axis=1) / (steps * SIDE)
    part_twist = np.stack([np.tile(t, (PARTS, 1)) for t in cis(few + 0.25, k, steps * SIDE)])
    part_dft = np.concatenate([rows, back_rows], axis=0)
    bf16, f32 = ml_dtypes.bfloat16, np.float32
    return dft.astype(bf16), twist.astype(f32), part_dft.astype(bf16), part_twist.astype(f32)


def steps_of(n):
    side = math.isqrt(n)
    steps = [(a, b) for a in range(side) for b in range(side) if a or b]
    return sorted(steps, key=lambda step: -sum(min(s, side - s) for s in step))


def kernel(
    n,
    proj_hbm, filt_hbm, taps_hbm, dft_hbm, twist_hbm, part_dft_hbm, part_twist_hbm,
    out,
    proj, filt, taps_ref, dft, twist, part_dft, part_twist, gate, stage, q_halo, head, sent, got, e_out, e_in, h_freq,
    load_sem, halo_send, halo_recv, sent_sem, back_sem, got_sem, e_send, e_recv, column_in,
):
    f32, bf16 = jnp.float32, jnp.bfloat16
    me = lax.axis_index("ctx")
    side = math.isqrt(n)
    my_row, my_column = me // side, lax.rem(me, side)

    def device(step):
        return lax.rem(my_row + step[0], side) * side + lax.rem(my_column + step[1], side)

    steps = steps_of(n)
    mates = [step for step in steps if not (step[0] and step[1])]
    width = filt.shape[1]
    tiles = width // LANES
    half = filt.shape[0] // 2

    barrier = pltpu.get_barrier_semaphore()
    for step in mates:
        pl.semaphore_signal(barrier, inc=1, device_id={"ctx": device(step)}, device_id_type=MESH)
    loads = [
        pltpu.make_async_copy(source, target, load_sem.at[at])
        for at, (source, target) in enumerate([
            (filt_hbm, filt), (taps_hbm, taps_ref), (proj_hbm, proj), (dft_hbm, dft), (twist_hbm, twist),
            (part_dft_hbm, part_dft), (part_twist_hbm, part_twist),
        ])
    ]
    for load in loads[:5]:
        load.start()

    @pl.when(me == 0)
    def _():
        for load in loads[5:]:
            load.start()

    whole = dft.at[0:SIDE], dft.at[SIDE : 2 * SIDE], twist
    part = part_dft.at[0:SIDE], part_dft.at[SIDE : 2 * SIDE], part_twist
    columns, back_columns = dft.at[2 * SIDE : 4 * SIDE], dft.at[4 * SIDE : 6 * SIDE]
    filters, mixes, results = (0, 2), (1, 3), (4, 5)

    def block(ref, at):
        return ref.at[pl.ds(at, 1)]

    def remote(source, target, send_sem, recv_sem, peer):
        return pltpu.make_async_remote_copy(
            src_ref=source, dst_ref=target, send_sem=send_sem, recv_sem=recv_sem,
            device_id={"ctx": peer}, device_id_type=MESH,
        )

    def send(at, chosen):
        for step in chosen:
            peer = device(step)
            remote(block(sent.at[at], peer), block(got.at[at], me), sent_sem, got_sem.at[at], peer).start()

    def send_back(at):
        for step in steps:
            peer = device(step)

            @pl.when(peer != 0)
            def _():
                remote(block(sent.at[at], peer), block(got.at[at], me), back_sem, got_sem.at[at], peer).start()

        @pl.when(me != 0)
        def _():
            keep(sent.at[at], got.at[at])

    def send_edges(chosen):
        for step in chosen:
            peer = device(step)
            remote(block(e_out, peer), block(e_in, me), e_send, e_recv, peer).start()

    def keep(source, target):
        target[pl.ds(me, 1)] = source[pl.ds(me, 1)]

    def others(ref, send_sem, recv_sem):
        part = ref.at[pl.ds(0, n - 1)]
        return remote(part, part, send_sem, recv_sem, me)

    def arrived(at):
        others(got.at[at], got_sem.at[at], got_sem.at[at]).wait_recv()

    def spread(value, group, tile_row, parity):
        stage[parity, pl.ds(group * 8 * 16 + tile_row, 8, stride=16), :] = value

    def gathered(target):
        for parity in range(2):
            target[:, :, LANES * parity : LANES * (parity + 1)] = stage[parity].astype(bf16).reshape(n, 16, LANES)

    def place_filter(j):
        def tile_pair(row, carry):
            for parity in range(2):
                at = pl.multiple_of((2 * row + parity) * LANES, LANES)
                value = filt[half * j : half * (j + 1), pl.ds(at, LANES)].astype(f32)
                for group in range(2):
                    spread(value[8 * group : 8 * group + 8], group, row, parity)
            return carry

        lax.fori_loop(0, tiles // 2, tile_pair, 0, unroll=True)
        gathered(sent.at[filters[j]])
        keep(sent.at[filters[j]], got.at[filters[j]])

    diagonal = lax.broadcasted_iota(jnp.int32, (half, 2 * half), 0)
    along = lax.broadcasted_iota(jnp.int32, (half, 2 * half), 1)
    lane = lax.broadcasted_iota(jnp.int32, (half, LANES), 1)
    lag_range, zero = range(3), jnp.zeros((half, LANES), f32)

    def tap(stream, lag, j):
        row = jnp.broadcast_to(taps_ref[stream, lag, :][None, :], (half, 2 * half))
        column = jnp.sum(jnp.where(along == diagonal + half * j, row, 0.0), axis=1, keepdims=True)
        return jnp.broadcast_to(column, (half, LANES))

    def own_tap(stream, lag, j):
        row = jnp.broadcast_to(taps_ref[stream, lag, :][None, :], (half, 2 * half))
        column = jnp.sum(jnp.where(along == me + half * j, row, 0.0), axis=1, keepdims=True)
        return jnp.broadcast_to(column, (half, LANES))

    def rolled(value):
        return value, pltpu.roll(value, 1, 1), pltpu.roll(value, 2, 1)

    def tile_of(stream, at, j):
        start = pl.multiple_of(at * LANES, LANES)
        return rolled(proj[stream, half * j : half * (j + 1), pl.ds(start, LANES)].astype(f32))

    def short(taps, now, before):
        one = jnp.where(lane < 1, before[1], now[1])
        two = jnp.where(lane < 2, before[2], now[2])
        return taps[0] * now[0] + taps[1] * one + taps[2] * two

    def place_mixed(j):
        taps = [[tap(stream, lag, j) for lag in lag_range] for stream in (1, 2)]

        def one_tile(row, parity, now, before):
            value = short(taps[0], now[0], before[0]) * short(taps[1], now[1], before[1])
            for group in range(2):
                spread(value[8 * group : 8 * group + 8], group, row, parity)

        def tile_pair(row, before):
            for parity in range(2):
                now = [tile_of(stream, 2 * row + parity, j) for stream in (1, 2)]
                one_tile(row, parity, now, before)
                before = now
            return before

        lax.fori_loop(0, tiles // 2, tile_pair, [(zero, zero, zero)] * 2, unroll=True)
        gathered(sent.at[mixes[j]])
        keep(sent.at[mixes[j]], got.at[mixes[j]])

    def place_edges():
        edges = zero
        for g in range(4):
            channels = slice(half * (g // 2), half * (g // 2) + half)
            first = proj[1 + g % 2, channels, 0:LANES].astype(f32)
            last = proj[1 + g % 2, channels, width - LANES : width].astype(f32)
            edges = jnp.where((lane >= 32 * g) & (lane < 32 * g + 16), pltpu.roll(first, 32 * g, 1) if g else first, edges)
            edges = jnp.where(
                (lane >= 32 * g + 16) & (lane < 32 * g + 32), pltpu.roll(last, 32 * (g + 1), 1) if g < 3 else last, edges
            )
        e_out[...] = edges[:, None, :]
        keep(e_out, e_in)

    def place_heads():
        edges = e_in[...].reshape(n, LANES)
        earlier = jnp.where(lax.broadcasted_iota(jnp.int32, (n, LANES), 0) < 1, 0.0, pltpu.roll(edges, 1, 0))
        for j in range(2):
            product = None
            for stream in (1, 2):
                g = 2 * j + stream - 1
                now = pltpu.roll(edges, LANES - 32 * g, 1) if g else edges
                one = jnp.where(lane < 1, pltpu.roll(earlier, (2 * LANES - 32 * g - 31) % LANES, 1), pltpu.roll(now, 1, 1))
                two = pltpu.roll(earlier, (2 * LANES - 32 * g - 30) % LANES, 1)
                taps = [own_tap(stream, lag, j) for lag in lag_range]
                value = taps[0] * now + taps[1] * one + taps[2] * two
                product = value if product is None else product * value
            for group in range(2):
                head[j, pl.ds(group * 8 * 16, 8, stride=16), :] = product[8 * group : 8 * group + 8]

    def mixed_of(j):
        at_row = lax.broadcasted_iota(jnp.int32, (SIDE, LANES), 0)
        at_lane = lax.broadcasted_iota(jnp.int32, (SIDE, LANES), 1)
        is_head = (lax.rem(at_row, 16) == 0) & (at_lane < 2)
        value = got[mixes[j]].reshape(SIDE, SIDE)
        even = jnp.where(is_head, head[j], value[:, 0:LANES].astype(f32)).astype(bf16)
        return jnp.concatenate([even, value[:, LANES:SIDE]], axis=1)

    def place_gate(j):
        taps = [tap(0, lag, j) for lag in lag_range]

        def tile(at, before):
            now = tile_of(0, at, j)
            gate[half * j : half * (j + 1), pl.ds(pl.multiple_of(at * LANES, LANES), LANES)] = short(taps, now, before)
            return now

        before = rolled(jnp.where(me > 0, q_halo[half * j : half * (j + 1), :].astype(f32), 0.0))
        lax.fori_loop(0, tiles, tile, before, unroll=True)

    def dot(a, b):
        return jnp.dot(a, b, preferred_element_type=f32)

    def forward(values, of):
        rows, _, twist = of
        values = jnp.concatenate(values, axis=1)
        reals, imags = dot(rows[:, :SIDE], values), dot(rows[:, SIDE:], values)
        cos, sin = twist[0], twist[1]
        turned = []
        for at in range(values.shape[1] // SIDE):
            own = slice(SIDE * at, SIDE * (at + 1))
            real, imag = reals[:, own], imags[:, own]
            turned.append(
                jnp.concatenate([(real * cos + imag * sin).astype(bf16), (imag * cos - real * sin).astype(bf16)], axis=1)
            )
        return dot(jnp.concatenate(turned, axis=0), columns[...])

    def convolved(x, h, of):
        _, back_rows, twist = of
        x_re, x_im, h_re, h_im = x[:, :SIDE], x[:, SIDE:], h[:, :SIDE], h[:, SIDE:]
        product = jnp.concatenate(
            [(x_re * h_re - x_im * h_im).astype(bf16), (x_re * h_im + x_im * h_re).astype(bf16)], axis=1
        )
        values = dot(product, back_columns[...])
        real, imag = values[:, :SIDE], values[:, SIDE:]
        cos, sin = twist[0], twist[1]
        turned = jnp.concatenate(
            [(real * cos - imag * sin).astype(bf16), (imag * cos + real * sin).astype(bf16)], axis=0
        )
        return dot(back_rows[...], turned).astype(bf16).reshape(n, 16, SIDE)

    def filter_of(j):
        return got[filters[j]].reshape(SIDE, SIDE)

    loads[0].wait()
    place_filter(0)
    place_filter(1)
    loads[1].wait()
    loads[2].wait()
    place_edges()
    pl.semaphore_wait(barrier, len(mates))
    for step in mates:
        if step[0]:
            pl.semaphore_signal(
                column_in.at[side - 1 - step[0]], inc=1, device_id={"ctx": device(step)}, device_id_type=MESH
            )
    send(filters[0], mates)
    place_mixed(0)
    send_edges(mates)
    send(mixes[0], mates)
    send(filters[1], mates)
    place_mixed(1)
    send(mixes[1], mates)
    for far in (1, side - 1, 2):
        pl.semaphore_wait(column_in.at[far - 1], 1)
        chosen = [step for step in steps if step[0] == far and step[1]]
        send(filters[0], chosen)
        send_edges(chosen)
        send(mixes[0], chosen)
    chosen = [step for step in steps if step[0] and step[1]]
    send(filters[1], chosen)
    send(mixes[1], chosen)
    last = proj.at[0, :, pl.ds(width - LANES, LANES)]
    halo = remote(last, q_halo, halo_send, halo_recv, lax.rem(me + 1, n))
    halo.start()
    for load in loads[3:5]:
        load.wait()

    @pl.when(me == 0)
    def _():
        for load in loads[5:]:
            load.wait()
        for j in range(2):
            both = forward([sent[at[j]].reshape(SIDE, SIDE) for at in (mixes, filters)], part)
            got[results[j]] = convolved(both[:SIDE], both[SIDE:], part)

    arrived(filters[0])
    h_freq[...] = forward([filter_of(0)], whole)
    others(e_in, e_recv, e_recv).wait_recv()
    place_heads()
    arrived(mixes[0])
    sent[results[0]] = convolved(forward([mixed_of(0)], whole), h_freq[...], whole)
    send_back(results[0])
    arrived(filters[1])
    arrived(mixes[1])
    both = forward([mixed_of(1), filter_of(1)], whole)
    sent[results[1]] = convolved(both[:SIDE], both[SIDE:], whole)
    send_back(results[1])

    halo.wait_recv()
    place_gate(0)
    place_gate(1)

    for j in range(2):
        @pl.when(me != 0)
        def _():
            arrived(results[j])

        stage[0] = got[results[j], :, :, 0:LANES].astype(f32).reshape(SIDE, LANES)
        stage[1] = got[results[j], :, :, LANES:SIDE].astype(f32).reshape(SIDE, LANES)

        def tile_pair(row, carry):
            for parity in range(2):
                at = pl.multiple_of((2 * row + parity) * LANES, LANES)
                value = jnp.concatenate(
                    [stage[parity, pl.ds(group * 8 * 16 + row, 8, stride=16), :] for group in range(2)], axis=0
                )
                value = value * gate[half * j : half * (j + 1), pl.ds(at, LANES)]
                out[half * j : half * (j + 1), pl.ds(at, LANES)] = value.astype(bf16)
            return carry

        lax.fori_loop(0, tiles // 2, tile_pair, 0, unroll=True)

    halo.wait_send()
    others(e_out, e_send, e_send).wait_send()

    def all_sent(ref, sem):
        remote(ref, ref, sem, sem, me).wait_send()

    all_sent(sent.at[0:4, 0 : n - 1], sent_sem)

    @pl.when(me == 0)
    def _():
        all_sent(sent.at[4:6, 0 : n - 1], back_sem)

    @pl.when(me != 0)
    def _():
        all_sent(sent.at[4:6, 0 : n - 2], back_sem)


def shards(n, projections, short_taps, long_filter):
    channels, width = long_filter.shape
    f32, bf16 = jnp.float32, jnp.bfloat16
    outside = pl.BlockSpec(memory_space=pltpu.HBM)
    inside = pl.BlockSpec(memory_space=pltpu.VMEM)
    edges = pltpu.VMEM((n, 1, LANES), f32)
    parts = pltpu.VMEM((6, n, SIDE // n, SIDE), bf16)
    one = pltpu.SemaphoreType.DMA
    operands = [projections, long_filter, short_taps, *(jnp.asarray(t) for t in tables())]
    return pl.pallas_call(
        functools.partial(kernel, n),
        out_shape=jax.ShapeDtypeStruct((channels, width), bf16),
        in_specs=[outside] * len(operands),
        out_specs=inside,
        scratch_shapes=[
            pltpu.VMEM((3, channels, width), bf16),
            pltpu.VMEM((channels, width), bf16),
            pltpu.VMEM((3, 3, channels), f32),
            pltpu.VMEM((6 * SIDE, 2 * SIDE), bf16),
            pltpu.VMEM((2, SIDE, SIDE), f32),
            pltpu.VMEM((2 * SIDE, 2 * SIDE), bf16),
            pltpu.VMEM((2, SIDE, SIDE), f32),
            pltpu.VMEM((channels, width), f32),
            pltpu.VMEM((2, SIDE, LANES), f32),
            pltpu.VMEM((channels, LANES), bf16),
            pltpu.VMEM((2, SIDE, LANES), f32),
            parts, parts, edges, edges,
            pltpu.VMEM((SIDE, 2 * SIDE), f32),
            pltpu.SemaphoreType.DMA((len(operands),)),
            one, one, one, one,
            pltpu.SemaphoreType.DMA((6,)),
            one, one,
            pltpu.SemaphoreType.REGULAR((math.isqrt(n) - 1,)),
        ],
        compiler_params=pltpu.CompilerParams(
            collective_id=0, has_side_effects=True, vmem_limit_bytes=32 * 1024 * 1024
        ),
        name="long_convolution",
    )(*(pltpu.with_memory_space_constraint(x, pltpu.HBM) for x in operands))


def solution(mesh):
    in_specs = (P(None, "chan", "ctx"), P(None, None, "chan"), P("chan", "ctx"))
    return jax.shard_map(
        functools.partial(shards, mesh.shape["ctx"]),
        mesh=mesh, in_specs=in_specs, out_specs=P("chan", "ctx"), check_vma=False,
    )
```

```python
import functools
import math

import jax
import jax.numpy as jnp
import ml_dtypes
import numpy as np
from jax import lax
from jax.experimental import pallas as pl
from jax.experimental.pallas import tpu as pltpu
from jax.sharding import PartitionSpec as P

MESH = pl.DeviceIdType.MESH
LANES = 128
SIDE = 256
TOTAL = SIDE * SIDE
PARTS = 16


def tables():
    k = np.arange(SIDE, dtype=np.float64)

    def cis(a, b, length):
        angle = 2.0 * np.pi * np.fmod(a[:, None] * b[None, :], length) / length
        return np.cos(angle), np.sin(angle)

    cos, sin = cis(k + 0.25, k, SIDE)
    rows = np.concatenate([cos, -sin], axis=1)
    back_rows = np.concatenate([cos.T, -sin.T], axis=1) / TOTAL
    twist = np.stack(cis(k + 0.25, k, TOTAL))
    cos, sin = cis(k, k, SIDE)
    columns = np.block([[cos, -sin], [sin, cos]])
    back_columns = np.block([[cos, sin], [-sin, cos]])
    dft = [rows, back_rows, columns, back_columns]

    steps = SIDE // PARTS
    few = np.arange(steps, dtype=np.float64)
    cos, sin = cis(few + 0.25, few, steps)
    every = np.eye(PARTS)
    rows = np.concatenate([np.kron(every, cos), np.kron(every, -sin)], axis=1)
    back_rows = np.concatenate([np.kron(every, cos.T), np.kron(every, -sin.T)], axis=1) / (steps * SIDE)
    part_twist = np.stack([np.tile(t, (PARTS, 1)) for t in cis(few + 0.25, k, steps * SIDE)])
    dft = np.concatenate(dft + [rows, back_rows], axis=0)
    return dft.astype(ml_dtypes.bfloat16), np.concatenate([twist, part_twist]).astype(np.float32)


def steps_of(n):
    side = math.isqrt(n)
    steps = [(a, b) for a in range(side) for b in range(side) if a or b]
    return sorted(steps, key=lambda step: -sum(min(s, side - s) for s in step))


def kernel(
    n,
    proj_hbm, filt_hbm, taps_hbm, dft_hbm, twist_hbm,
    out,
    proj, filt, taps_ref, dft, twists, gate, stage, q_halo, head, sent, got, e_out, e_in, h_freq,
    load_sem, halo_send, halo_recv, sent_sem, back_sem, got_sem, e_send, e_recv, column_in,
):
    f32, bf16 = jnp.float32, jnp.bfloat16
    me = lax.axis_index("ctx")
    side = math.isqrt(n)
    my_row, my_column = me // side, lax.rem(me, side)

    def device(step):
        return lax.rem(my_row + step[0], side) * side + lax.rem(my_column + step[1], side)

    steps = steps_of(n)
    mates = [step for step in steps if not (step[0] and step[1])]
    width = filt.shape[1]
    tiles = width // LANES
    half = filt.shape[0] // 2

    barrier = pltpu.get_barrier_semaphore()
    for step in mates:
        pl.semaphore_signal(barrier, inc=1, device_id={"ctx": device(step)}, device_id_type=MESH)
    loads = [
        pltpu.make_async_copy(source, target, load_sem.at[at])
        for at, (source, target) in enumerate([
            (filt_hbm, filt), (taps_hbm, taps_ref), (proj_hbm, proj), (dft_hbm, dft), (twist_hbm, twists),
        ])
    ]
    for load in loads:
        load.start()
    whole = dft.at[0:SIDE], dft.at[SIDE : 2 * SIDE], twists.at[0:2]
    part = dft.at[6 * SIDE : 7 * SIDE], dft.at[7 * SIDE : 8 * SIDE], twists.at[2:4]
    columns, back_columns = dft.at[2 * SIDE : 4 * SIDE], dft.at[4 * SIDE : 6 * SIDE]
    filters, mixes, results = (0, 2), (1, 3), (4, 5)

    def block(ref, at):
        return ref.at[pl.ds(at, 1)]

    def remote(source, target, send_sem, recv_sem, peer):
        return pltpu.make_async_remote_copy(
            src_ref=source, dst_ref=target, send_sem=send_sem, recv_sem=recv_sem,
            device_id={"ctx": peer}, device_id_type=MESH,
        )

    def send(at, chosen):
        for step in chosen:
            peer = device(step)
            remote(block(sent.at[at], peer), block(got.at[at], me), sent_sem, got_sem.at[min(at, 2)], peer).start()

    def send_back(at):
        for step in steps:
            peer = device(step)

            @pl.when(peer != 0)
            def _():
                remote(block(sent.at[at], peer), block(got.at[at], me), back_sem, got_sem.at[at - 1], peer).start()

        @pl.when(me != 0)
        def _():
            keep(sent.at[at], got.at[at])

    def send_edges(chosen):
        for step in chosen:
            peer = device(step)
            remote(block(e_out, peer), block(e_in, me), e_send, e_recv, peer).start()

    def keep(source, target):
        target[pl.ds(me, 1)] = source[pl.ds(me, 1)]

    def others(ref, send_sem, recv_sem):
        part = ref.at[pl.ds(0, n - 1)]
        return remote(part, part, send_sem, recv_sem, me)

    def arrived(at, sem):
        others(got.at[at], got_sem.at[sem], got_sem.at[sem]).wait_recv()

    def spread(value, group, tile_row, parity):
        stage[parity, pl.ds(group * 8 * 16 + tile_row, 8, stride=16), :] = value

    def gathered(target):
        for parity in range(2):
            target[:, :, LANES * parity : LANES * (parity + 1)] = stage[parity].astype(bf16).reshape(n, 16, LANES)

    def place_filter(j):
        def tile_pair(row, carry):
            for parity in range(2):
                at = pl.multiple_of((2 * row + parity) * LANES, LANES)
                value = filt[half * j : half * (j + 1), pl.ds(at, LANES)].astype(f32)
                for group in range(2):
                    spread(value[8 * group : 8 * group + 8], group, row, parity)
            return carry

        lax.fori_loop(0, tiles // 2, tile_pair, 0, unroll=True)
        gathered(sent.at[filters[j]])
        keep(sent.at[filters[j]], got.at[filters[j]])

    diagonal = lax.broadcasted_iota(jnp.int32, (half, 2 * half), 0)
    along = lax.broadcasted_iota(jnp.int32, (half, 2 * half), 1)
    lane = lax.broadcasted_iota(jnp.int32, (half, LANES), 1)
    lag_range, zero = range(3), jnp.zeros((half, LANES), f32)

    def tap(stream, lag, j):
        row = jnp.broadcast_to(taps_ref[stream, lag, :][None, :], (half, 2 * half))
        column = jnp.sum(jnp.where(along == diagonal + half * j, row, 0.0), axis=1, keepdims=True)
        return jnp.broadcast_to(column, (half, LANES))

    def own_tap(stream, lag, j):
        row = jnp.broadcast_to(taps_ref[stream, lag, :][None, :], (half, 2 * half))
        column = jnp.sum(jnp.where(along == me + half * j, row, 0.0), axis=1, keepdims=True)
        return jnp.broadcast_to(column, (half, LANES))

    def rolled(value):
        return value, pltpu.roll(value, 1, 1), pltpu.roll(value, 2, 1)

    def tile_of(stream, at, j):
        start = pl.multiple_of(at * LANES, LANES)
        return rolled(proj[stream, half * j : half * (j + 1), pl.ds(start, LANES)].astype(f32))

    def short(taps, now, before):
        one = jnp.where(lane < 1, before[1], now[1])
        two = jnp.where(lane < 2, before[2], now[2])
        return taps[0] * now[0] + taps[1] * one + taps[2] * two

    def place_mixed(j):
        taps = [[tap(stream, lag, j) for lag in lag_range] for stream in (1, 2)]

        def one_tile(row, parity, now, before):
            value = short(taps[0], now[0], before[0]) * short(taps[1], now[1], before[1])
            for group in range(2):
                spread(value[8 * group : 8 * group + 8], group, row, parity)

        def tile_pair(row, before):
            for parity in range(2):
                now = [tile_of(stream, 2 * row + parity, j) for stream in (1, 2)]
                one_tile(row, parity, now, before)
                before = now
            return before

        lax.fori_loop(0, tiles // 2, tile_pair, [(zero, zero, zero)] * 2, unroll=True)
        gathered(sent.at[mixes[j]])
        keep(sent.at[mixes[j]], got.at[mixes[j]])

    def place_edges():
        edges = zero
        for g in range(4):
            channels = slice(half * (g // 2), half * (g // 2) + half)
            first = proj[1 + g % 2, channels, 0:LANES].astype(f32)
            last = proj[1 + g % 2, channels, width - LANES : width].astype(f32)
            edges = jnp.where((lane >= 32 * g) & (lane < 32 * g + 16), pltpu.roll(first, 32 * g, 1) if g else first, edges)
            edges = jnp.where(
                (lane >= 32 * g + 16) & (lane < 32 * g + 32), pltpu.roll(last, 32 * (g + 1), 1) if g < 3 else last, edges
            )
        e_out[...] = edges[:, None, :]
        keep(e_out, e_in)

    def place_heads():
        edges = e_in[...].reshape(n, LANES)
        earlier = jnp.where(lax.broadcasted_iota(jnp.int32, (n, LANES), 0) < 1, 0.0, pltpu.roll(edges, 1, 0))
        for j in range(2):
            product = None
            for stream in (1, 2):
                g = 2 * j + stream - 1
                now = pltpu.roll(edges, LANES - 32 * g, 1) if g else edges
                one = jnp.where(lane < 1, pltpu.roll(earlier, (2 * LANES - 32 * g - 31) % LANES, 1), pltpu.roll(now, 1, 1))
                two = pltpu.roll(earlier, (2 * LANES - 32 * g - 30) % LANES, 1)
                taps = [own_tap(stream, lag, j) for lag in lag_range]
                value = taps[0] * now + taps[1] * one + taps[2] * two
                product = value if product is None else product * value
            for group in range(2):
                head[j, pl.ds(group * 8 * 16, 8, stride=16), :] = product[8 * group : 8 * group + 8]

    def mixed_of(j):
        at_row = lax.broadcasted_iota(jnp.int32, (SIDE, LANES), 0)
        at_lane = lax.broadcasted_iota(jnp.int32, (SIDE, LANES), 1)
        is_head = (lax.rem(at_row, 16) == 0) & (at_lane < 2)
        value = got[mixes[j]].reshape(SIDE, SIDE)
        even = jnp.where(is_head, head[j], value[:, 0:LANES].astype(f32)).astype(bf16)
        return jnp.concatenate([even, value[:, LANES:SIDE]], axis=1)

    def place_gate(j):
        taps = [tap(0, lag, j) for lag in lag_range]

        def tile(at, before):
            now = tile_of(0, at, j)
            gate[half * j : half * (j + 1), pl.ds(pl.multiple_of(at * LANES, LANES), LANES)] = short(taps, now, before)
            return now

        before = rolled(jnp.where(me > 0, q_halo[half * j : half * (j + 1), :].astype(f32), 0.0))
        lax.fori_loop(0, tiles, tile, before, unroll=True)

    def dot(a, b):
        return jnp.dot(a, b, preferred_element_type=f32)

    def forward(values, of):
        rows, _, twist = of
        values = jnp.concatenate(values, axis=1)
        reals, imags = dot(rows[:, :SIDE], values), dot(rows[:, SIDE:], values)
        cos, sin = twist[0], twist[1]
        turned = []
        for at in range(values.shape[1] // SIDE):
            own = slice(SIDE * at, SIDE * (at + 1))
            real, imag = reals[:, own], imags[:, own]
            turned.append(
                jnp.concatenate([(real * cos + imag * sin).astype(bf16), (imag * cos - real * sin).astype(bf16)], axis=1)
            )
        return dot(jnp.concatenate(turned, axis=0), columns[...])

    def convolved(x, h, of):
        _, back_rows, twist = of
        x_re, x_im, h_re, h_im = x[:, :SIDE], x[:, SIDE:], h[:, :SIDE], h[:, SIDE:]
        product = jnp.concatenate(
            [(x_re * h_re - x_im * h_im).astype(bf16), (x_re * h_im + x_im * h_re).astype(bf16)], axis=1
        )
        values = dot(product, back_columns[...])
        real, imag = values[:, :SIDE], values[:, SIDE:]
        cos, sin = twist[0], twist[1]
        turned = jnp.concatenate(
            [(real * cos - imag * sin).astype(bf16), (imag * cos + real * sin).astype(bf16)], axis=0
        )
        return dot(back_rows[...], turned).astype(bf16).reshape(n, 16, SIDE)

    def filter_of(j):
        return got[filters[j]].reshape(SIDE, SIDE)

    loads[0].wait()
    place_filter(0)
    place_filter(1)
    loads[1].wait()
    loads[2].wait()
    place_edges()
    pl.semaphore_wait(barrier, len(mates))
    for step in mates:
        if step[0]:
            pl.semaphore_signal(
                column_in.at[side - 1 - step[0]], inc=1, device_id={"ctx": device(step)}, device_id_type=MESH
            )
    send_edges(mates)
    send(filters[0], mates)
    place_mixed(0)
    send(mixes[0], mates)
    send(filters[1], [step for step in mates if 2 not in step])
    place_mixed(1)
    send(mixes[1], [step for step in mates if 2 not in step])
    for far in (1, side - 1, 2):
        pl.semaphore_wait(column_in.at[far - 1], 1)
        chosen = [step for step in steps if step[0] == far and step[1]]
        send_edges(chosen)
        send(filters[0], chosen)
        send(mixes[0], chosen)
    chosen = [step for step in steps if step[0] and step[1]]
    send(filters[1], chosen)
    send(mixes[1], chosen)
    send(filters[1], [step for step in mates if 2 in step])
    send(mixes[1], [step for step in mates if 2 in step])
    last = proj.at[0, :, pl.ds(width - LANES, LANES)]
    halo = remote(last, q_halo, halo_send, halo_recv, lax.rem(me + 1, n))
    halo.start()
    for load in loads[3:]:
        load.wait()

    @pl.when(me == 0)
    def _():
        for j in range(2):
            both = forward([sent[at[j]].reshape(SIDE, SIDE) for at in (mixes, filters)], part)
            got[results[j]] = convolved(both[:SIDE], both[SIDE:], part)

    others(e_in, e_recv, e_recv).wait_recv()
    arrived(filters[0], 0)
    place_heads()
    h_freq[...] = forward([filter_of(0)], whole)
    arrived(mixes[0], 1)
    sent[results[0]] = convolved(forward([mixed_of(0)], whole), h_freq[...], whole)
    send_back(results[0])
    pair = got.at[filters[1] : mixes[1] + 1, 0 : n - 1]
    remote(pair, pair, got_sem.at[2], got_sem.at[2], me).wait_recv()
    both = forward([mixed_of(1), filter_of(1)], whole)
    sent[results[1]] = convolved(both[:SIDE], both[SIDE:], whole)
    send_back(results[1])

    halo.wait_recv()
    place_gate(0)
    place_gate(1)

    for j in range(2):
        @pl.when(me != 0)
        def _():
            arrived(results[j], 3 + j)

        stage[0] = got[results[j], :, :, 0:LANES].astype(f32).reshape(SIDE, LANES)
        stage[1] = got[results[j], :, :, LANES:SIDE].astype(f32).reshape(SIDE, LANES)

        def tile_pair(row, carry):
            for parity in range(2):
                at = pl.multiple_of((2 * row + parity) * LANES, LANES)
                value = jnp.concatenate(
                    [stage[parity, pl.ds(group * 8 * 16 + row, 8, stride=16), :] for group in range(2)], axis=0
                )
                value = value * gate[half * j : half * (j + 1), pl.ds(at, LANES)]
                out[half * j : half * (j + 1), pl.ds(at, LANES)] = value.astype(bf16)
            return carry

        lax.fori_loop(0, tiles // 2, tile_pair, 0, unroll=True)

    halo.wait_send()
    others(e_out, e_send, e_send).wait_send()

    def all_sent(ref, sem):
        remote(ref, ref, sem, sem, me).wait_send()

    all_sent(sent.at[0:4, 0 : n - 1], sent_sem)

    @pl.when(me == 0)
    def _():
        all_sent(sent.at[4:6, 0 : n - 1], back_sem)

    @pl.when(me != 0)
    def _():
        all_sent(sent.at[4:6, 0 : n - 2], back_sem)


def shards(n, projections, short_taps, long_filter):
    channels, width = long_filter.shape
    f32, bf16 = jnp.float32, jnp.bfloat16
    outside = pl.BlockSpec(memory_space=pltpu.HBM)
    inside = pl.BlockSpec(memory_space=pltpu.VMEM)
    edges = pltpu.VMEM((n, 1, LANES), f32)
    parts = pltpu.VMEM((6, n, SIDE // n, SIDE), bf16)
    one = pltpu.SemaphoreType.DMA
    operands = [projections, long_filter, short_taps, *(jnp.asarray(t) for t in tables())]
    return pl.pallas_call(
        functools.partial(kernel, n),
        out_shape=jax.ShapeDtypeStruct((channels, width), bf16),
        in_specs=[outside] * len(operands),
        out_specs=inside,
        scratch_shapes=[
            pltpu.VMEM((3, channels, width), bf16),
            pltpu.VMEM((channels, width), bf16),
            pltpu.VMEM((3, 3, channels), f32),
            pltpu.VMEM((8 * SIDE, 2 * SIDE), bf16),
            pltpu.VMEM((4, SIDE, SIDE), f32),
            pltpu.VMEM((channels, width), f32),
            pltpu.VMEM((2, SIDE, LANES), f32),
            pltpu.VMEM((channels, LANES), bf16),
            pltpu.VMEM((2, SIDE, LANES), f32),
            parts, parts, edges, edges,
            pltpu.VMEM((SIDE, 2 * SIDE), f32),
            pltpu.SemaphoreType.DMA((len(operands),)),
            one, one, one, one,
            pltpu.SemaphoreType.DMA((5,)),
            one, one,
            pltpu.SemaphoreType.REGULAR((math.isqrt(n) - 1,)),
        ],
        compiler_params=pltpu.CompilerParams(
            collective_id=0, has_side_effects=True, vmem_limit_bytes=32 * 1024 * 1024
        ),
        name="long_convolution",
    )(*(pltpu.with_memory_space_constraint(x, pltpu.HBM) for x in operands))


def solution(mesh):
    in_specs = (P(None, "chan", "ctx"), P(None, None, "chan"), P("chan", "ctx"))
    return jax.shard_map(
        functools.partial(shards, mesh.shape["ctx"]),
        mesh=mesh, in_specs=in_specs, out_specs=P("chan", "ctx"), check_vma=False,
    )
```

```python
import functools
import math

import jax
import jax.numpy as jnp
import ml_dtypes
import numpy as np
from jax import lax
from jax.experimental import pallas as pl
from jax.experimental.pallas import tpu as pltpu
from jax.sharding import PartitionSpec as P

MESH = pl.DeviceIdType.MESH
LANES = 128
SIDE = 256
TOTAL = SIDE * SIDE
PARTS = 16


def tables():
    k = np.arange(SIDE, dtype=np.float64)

    def cis(a, b, length):
        angle = 2.0 * np.pi * np.fmod(a[:, None] * b[None, :], length) / length
        return np.cos(angle), np.sin(angle)

    cos, sin = cis(k + 0.25, k, SIDE)
    rows = np.concatenate([cos, -sin], axis=1)
    back_rows = np.concatenate([cos.T, -sin.T], axis=1) / TOTAL
    twist = np.stack(cis(k + 0.25, k, TOTAL))
    cos, sin = cis(k, k, SIDE)
    columns = np.block([[cos, -sin], [sin, cos]])
    back_columns = np.block([[cos, sin], [-sin, cos]])
    dft = [rows, back_rows, columns, back_columns]

    steps = SIDE // PARTS
    few = np.arange(steps, dtype=np.float64)
    cos, sin = cis(few + 0.25, few, steps)
    every = np.eye(PARTS)
    rows = np.concatenate([np.kron(every, cos), np.kron(every, -sin)], axis=1)
    back_rows = np.concatenate([np.kron(every, cos.T), np.kron(every, -sin.T)], axis=1) / (steps * SIDE)
    part_twist = np.stack([np.tile(t, (PARTS, 1)) for t in cis(few + 0.25, k, steps * SIDE)])
    dft = np.concatenate(dft + [rows, back_rows], axis=0)
    return dft.astype(ml_dtypes.bfloat16), np.concatenate([twist, part_twist]).astype(np.float32)


def steps_of(n):
    side = math.isqrt(n)
    steps = [(a, b) for a in range(side) for b in range(side) if a or b]
    return sorted(steps, key=lambda step: -sum(min(s, side - s) for s in step))


def kernel(
    n,
    proj_hbm, filt_hbm, taps_hbm, dft_hbm, twist_hbm,
    out,
    proj, filt, taps_ref, dft, twists, gate, stage, q_halo, head, sent, got, e_out, e_in, h_freq,
    load_sem, halo_send, halo_recv, sent_sem, back_sem, got_sem, e_send, e_recv, column_in,
):
    f32, bf16 = jnp.float32, jnp.bfloat16
    me = lax.axis_index("ctx")
    side = math.isqrt(n)
    my_row, my_column = me // side, lax.rem(me, side)

    def device(step):
        return lax.rem(my_row + step[0], side) * side + lax.rem(my_column + step[1], side)

    steps = steps_of(n)
    mates = [step for step in steps if not (step[0] and step[1])]
    width = filt.shape[1]
    tiles = width // LANES
    half = filt.shape[0] // 2

    barrier = pltpu.get_barrier_semaphore()
    for step in mates:
        pl.semaphore_signal(barrier, inc=1, device_id={"ctx": device(step)}, device_id_type=MESH)
    loads = [
        pltpu.make_async_copy(source, target, load_sem.at[at])
        for at, (source, target) in enumerate([
            (filt_hbm, filt), (taps_hbm, taps_ref), (proj_hbm, proj), (dft_hbm, dft), (twist_hbm, twists),
        ])
    ]
    for load in loads[:3]:
        load.start()
    whole = dft.at[0:SIDE], dft.at[SIDE : 2 * SIDE], twists.at[0:2]
    part = dft.at[6 * SIDE : 7 * SIDE], dft.at[7 * SIDE : 8 * SIDE], twists.at[2:4]
    columns, back_columns = dft.at[2 * SIDE : 4 * SIDE], dft.at[4 * SIDE : 6 * SIDE]
    filters, mixes, results = (0, 2), (1, 3), (4, 5)

    def block(ref, at):
        return ref.at[pl.ds(at, 1)]

    def remote(source, target, send_sem, recv_sem, peer):
        return pltpu.make_async_remote_copy(
            src_ref=source, dst_ref=target, send_sem=send_sem, recv_sem=recv_sem,
            device_id={"ctx": peer}, device_id_type=MESH,
        )

    def send(at, chosen):
        for step in chosen:
            peer = device(step)
            remote(block(sent.at[at], peer), block(got.at[at], me), sent_sem, got_sem.at[min(at, 2)], peer).start()

    def send_back(at):
        for step in steps:
            peer = device(step)

            @pl.when(peer != 0)
            def _():
                remote(block(sent.at[at], peer), block(got.at[at], me), back_sem, got_sem.at[at - 1], peer).start()

        @pl.when(me != 0)
        def _():
            keep(sent.at[at], got.at[at])

    def send_edges(chosen):
        for step in chosen:
            peer = device(step)
            remote(block(e_out, peer), block(e_in, me), e_send, e_recv, peer).start()

    def keep(source, target):
        target[pl.ds(me, 1)] = source[pl.ds(me, 1)]

    def others(ref, send_sem, recv_sem):
        part = ref.at[pl.ds(0, n - 1)]
        return remote(part, part, send_sem, recv_sem, me)

    def arrived(at, sem):
        others(got.at[at], got_sem.at[sem], got_sem.at[sem]).wait_recv()

    def spread(value, group, tile_row, parity):
        stage[parity, pl.ds(group * 8 * 16 + tile_row, 8, stride=16), :] = value

    def gathered(target):
        for parity in range(2):
            target[:, :, LANES * parity : LANES * (parity + 1)] = stage[parity].astype(bf16).reshape(n, 16, LANES)

    def place_filter(j):
        def tile_pair(row, carry):
            for parity in range(2):
                at = pl.multiple_of((2 * row + parity) * LANES, LANES)
                value = filt[half * j : half * (j + 1), pl.ds(at, LANES)].astype(f32)
                for group in range(2):
                    spread(value[8 * group : 8 * group + 8], group, row, parity)
            return carry

        lax.fori_loop(0, tiles // 2, tile_pair, 0, unroll=True)
        gathered(sent.at[filters[j]])
        keep(sent.at[filters[j]], got.at[filters[j]])

    diagonal = lax.broadcasted_iota(jnp.int32, (half, 2 * half), 0)
    along = lax.broadcasted_iota(jnp.int32, (half, 2 * half), 1)
    lane = lax.broadcasted_iota(jnp.int32, (half, LANES), 1)
    lag_range, zero = range(3), jnp.zeros((half, LANES), f32)

    def tap(stream, lag, j):
        row = jnp.broadcast_to(taps_ref[stream, lag, :][None, :], (half, 2 * half))
        column = jnp.sum(jnp.where(along == diagonal + half * j, row, 0.0), axis=1, keepdims=True)
        return jnp.broadcast_to(column, (half, LANES))

    def own_tap(stream, lag, j):
        row = jnp.broadcast_to(taps_ref[stream, lag, :][None, :], (half, 2 * half))
        column = jnp.sum(jnp.where(along == me + half * j, row, 0.0), axis=1, keepdims=True)
        return jnp.broadcast_to(column, (half, LANES))

    def rolled(value):
        return value, pltpu.roll(value, 1, 1), pltpu.roll(value, 2, 1)

    def tile_of(stream, at, j):
        start = pl.multiple_of(at * LANES, LANES)
        return rolled(proj[stream, half * j : half * (j + 1), pl.ds(start, LANES)].astype(f32))

    def short(taps, now, before):
        one = jnp.where(lane < 1, before[1], now[1])
        two = jnp.where(lane < 2, before[2], now[2])
        return taps[0] * now[0] + taps[1] * one + taps[2] * two

    def place_mixed(j):
        taps = [[tap(stream, lag, j) for lag in lag_range] for stream in (1, 2)]

        def one_tile(row, parity, now, before):
            value = short(taps[0], now[0], before[0]) * short(taps[1], now[1], before[1])
            for group in range(2):
                spread(value[8 * group : 8 * group + 8], group, row, parity)

        def tile_pair(row, before):
            for parity in range(2):
                now = [tile_of(stream, 2 * row + parity, j) for stream in (1, 2)]
                one_tile(row, parity, now, before)
                before = now
            return before

        lax.fori_loop(0, tiles // 2, tile_pair, [(zero, zero, zero)] * 2, unroll=True)
        gathered(sent.at[mixes[j]])
        keep(sent.at[mixes[j]], got.at[mixes[j]])

    def place_edges():
        edges = zero
        for g in range(4):
            channels = slice(half * (g // 2), half * (g // 2) + half)
            first = proj[1 + g % 2, channels, 0:LANES].astype(f32)
            last = proj[1 + g % 2, channels, width - LANES : width].astype(f32)
            edges = jnp.where((lane >= 32 * g) & (lane < 32 * g + 16), pltpu.roll(first, 32 * g, 1) if g else first, edges)
            edges = jnp.where(
                (lane >= 32 * g + 16) & (lane < 32 * g + 32), pltpu.roll(last, 32 * (g + 1), 1) if g < 3 else last, edges
            )
        e_out[...] = edges[:, None, :]
        keep(e_out, e_in)

    def place_heads():
        edges = e_in[...].reshape(n, LANES)
        earlier = jnp.where(lax.broadcasted_iota(jnp.int32, (n, LANES), 0) < 1, 0.0, pltpu.roll(edges, 1, 0))
        for j in range(2):
            product = None
            for stream in (1, 2):
                g = 2 * j + stream - 1
                now = pltpu.roll(edges, LANES - 32 * g, 1) if g else edges
                one = jnp.where(lane < 1, pltpu.roll(earlier, (2 * LANES - 32 * g - 31) % LANES, 1), pltpu.roll(now, 1, 1))
                two = pltpu.roll(earlier, (2 * LANES - 32 * g - 30) % LANES, 1)
                taps = [own_tap(stream, lag, j) for lag in lag_range]
                value = taps[0] * now + taps[1] * one + taps[2] * two
                product = value if product is None else product * value
            for group in range(2):
                head[j, pl.ds(group * 8 * 16, 8, stride=16), :] = product[8 * group : 8 * group + 8]

    def mixed_of(j):
        at_row = lax.broadcasted_iota(jnp.int32, (SIDE, LANES), 0)
        at_lane = lax.broadcasted_iota(jnp.int32, (SIDE, LANES), 1)
        is_head = (lax.rem(at_row, 16) == 0) & (at_lane < 2)
        value = got[mixes[j]].reshape(SIDE, SIDE)
        even = jnp.where(is_head, head[j], value[:, 0:LANES].astype(f32)).astype(bf16)
        return jnp.concatenate([even, value[:, LANES:SIDE]], axis=1)

    def place_gate(j):
        taps = [tap(0, lag, j) for lag in lag_range]

        def tile(at, before):
            now = tile_of(0, at, j)
            gate[half * j : half * (j + 1), pl.ds(pl.multiple_of(at * LANES, LANES), LANES)] = short(taps, now, before)
            return now

        before = rolled(jnp.where(me > 0, q_halo[half * j : half * (j + 1), :].astype(f32), 0.0))
        lax.fori_loop(0, tiles, tile, before, unroll=True)

    def dot(a, b):
        return jnp.dot(a, b, preferred_element_type=f32)

    def forward(values, of):
        rows, _, twist = of
        values = jnp.concatenate(values, axis=1)
        reals, imags = dot(rows[:, :SIDE], values), dot(rows[:, SIDE:], values)
        cos, sin = twist[0], twist[1]
        turned = []
        for at in range(values.shape[1] // SIDE):
            own = slice(SIDE * at, SIDE * (at + 1))
            real, imag = reals[:, own], imags[:, own]
            turned.append(
                jnp.concatenate([(real * cos + imag * sin).astype(bf16), (imag * cos - real * sin).astype(bf16)], axis=1)
            )
        return dot(jnp.concatenate(turned, axis=0), columns[...])

    def convolved(x, h, of):
        _, back_rows, twist = of
        x_re, x_im, h_re, h_im = x[:, :SIDE], x[:, SIDE:], h[:, :SIDE], h[:, SIDE:]
        product = jnp.concatenate(
            [(x_re * h_re - x_im * h_im).astype(bf16), (x_re * h_im + x_im * h_re).astype(bf16)], axis=1
        )
        values = dot(product, back_columns[...])
        real, imag = values[:, :SIDE], values[:, SIDE:]
        cos, sin = twist[0], twist[1]
        turned = jnp.concatenate(
            [(real * cos - imag * sin).astype(bf16), (imag * cos + real * sin).astype(bf16)], axis=0
        )
        return dot(back_rows[...], turned).astype(bf16).reshape(n, 16, SIDE)

    def filter_of(j):
        return got[filters[j]].reshape(SIDE, SIDE)

    loads[0].wait()
    place_filter(0)
    place_filter(1)
    loads[1].wait()
    loads[2].wait()
    for load in loads[3:]:
        load.start()
    place_edges()
    pl.semaphore_wait(barrier, len(mates))
    for step in mates:
        if step[0]:
            pl.semaphore_signal(
                column_in.at[side - 1 - step[0]], inc=1, device_id={"ctx": device(step)}, device_id_type=MESH
            )
    send_edges(mates)
    send(filters[0], mates)
    place_mixed(0)
    send(mixes[0], mates)
    send(filters[1], [step for step in mates if 2 not in step])
    place_mixed(1)
    send(mixes[1], [step for step in mates if 2 not in step])
    for far in (1, side - 1, 2):
        pl.semaphore_wait(column_in.at[far - 1], 1)
        chosen = [step for step in steps if step[0] == far and step[1]]
        send_edges(chosen)
        send(filters[0], chosen)
        send(mixes[0], chosen)
    chosen = [step for step in steps if step[0] and step[1]]
    send(filters[1], chosen)
    send(mixes[1], chosen)
    send(filters[1], [step for step in mates if 2 in step])
    send(mixes[1], [step for step in mates if 2 in step])
    last = proj.at[0, :, pl.ds(width - LANES, LANES)]
    halo = remote(last, q_halo, halo_send, halo_recv, lax.rem(me + 1, n))
    halo.start()
    for load in loads[3:]:
        load.wait()

    @pl.when(me == 0)
    def _():
        for j in range(2):
            both = forward([sent[at[j]].reshape(SIDE, SIDE) for at in (mixes, filters)], part)
            got[results[j]] = convolved(both[:SIDE], both[SIDE:], part)

    others(e_in, e_recv, e_recv).wait_recv()
    arrived(filters[0], 0)
    place_heads()
    h_freq[...] = forward([filter_of(0)], whole)
    arrived(mixes[0], 1)
    sent[results[0]] = convolved(forward([mixed_of(0)], whole), h_freq[...], whole)
    send_back(results[0])
    pair = got.at[filters[1] : mixes[1] + 1, 0 : n - 1]
    remote(pair, pair, got_sem.at[2], got_sem.at[2], me).wait_recv()
    both = forward([mixed_of(1), filter_of(1)], whole)
    sent[results[1]] = convolved(both[:SIDE], both[SIDE:], whole)
    send_back(results[1])

    halo.wait_recv()
    place_gate(0)
    place_gate(1)

    for j in range(2):
        @pl.when(me != 0)
        def _():
            arrived(results[j], 3 + j)

        stage[0] = got[results[j], :, :, 0:LANES].astype(f32).reshape(SIDE, LANES)
        stage[1] = got[results[j], :, :, LANES:SIDE].astype(f32).reshape(SIDE, LANES)

        def tile_pair(row, carry):
            for parity in range(2):
                at = pl.multiple_of((2 * row + parity) * LANES, LANES)
                value = jnp.concatenate(
                    [stage[parity, pl.ds(group * 8 * 16 + row, 8, stride=16), :] for group in range(2)], axis=0
                )
                value = value * gate[half * j : half * (j + 1), pl.ds(at, LANES)]
                out[half * j : half * (j + 1), pl.ds(at, LANES)] = value.astype(bf16)
            return carry

        lax.fori_loop(0, tiles // 2, tile_pair, 0, unroll=True)

    halo.wait_send()
    others(e_out, e_send, e_send).wait_send()

    def all_sent(ref, sem):
        remote(ref, ref, sem, sem, me).wait_send()

    all_sent(sent.at[0:4, 0 : n - 1], sent_sem)

    @pl.when(me == 0)
    def _():
        all_sent(sent.at[4:6, 0 : n - 1], back_sem)

    @pl.when(me != 0)
    def _():
        all_sent(sent.at[4:6, 0 : n - 2], back_sem)


def shards(n, projections, short_taps, long_filter):
    channels, width = long_filter.shape
    f32, bf16 = jnp.float32, jnp.bfloat16
    outside = pl.BlockSpec(memory_space=pltpu.HBM)
    inside = pl.BlockSpec(memory_space=pltpu.VMEM)
    edges = pltpu.VMEM((n, 1, LANES), f32)
    parts = pltpu.VMEM((6, n, SIDE // n, SIDE), bf16)
    one = pltpu.SemaphoreType.DMA
    operands = [projections, long_filter, short_taps, *(jnp.asarray(t) for t in tables())]
    return pl.pallas_call(
        functools.partial(kernel, n),
        out_shape=jax.ShapeDtypeStruct((channels, width), bf16),
        in_specs=[outside] * len(operands),
        out_specs=inside,
        scratch_shapes=[
            pltpu.VMEM((3, channels, width), bf16),
            pltpu.VMEM((channels, width), bf16),
            pltpu.VMEM((3, 3, channels), f32),
            pltpu.VMEM((8 * SIDE, 2 * SIDE), bf16),
            pltpu.VMEM((4, SIDE, SIDE), f32),
            pltpu.VMEM((channels, width), f32),
            pltpu.VMEM((2, SIDE, LANES), f32),
            pltpu.VMEM((channels, LANES), bf16),
            pltpu.VMEM((2, SIDE, LANES), f32),
            parts, parts, edges, edges,
            pltpu.VMEM((SIDE, 2 * SIDE), f32),
            pltpu.SemaphoreType.DMA((len(operands),)),
            one, one, one, one,
            pltpu.SemaphoreType.DMA((5,)),
            one, one,
            pltpu.SemaphoreType.REGULAR((math.isqrt(n) - 1,)),
        ],
        compiler_params=pltpu.CompilerParams(
            collective_id=0, has_side_effects=True, vmem_limit_bytes=32 * 1024 * 1024
        ),
        name="long_convolution",
    )(*(pltpu.with_memory_space_constraint(x, pltpu.HBM) for x in operands))


def solution(mesh):
    in_specs = (P(None, "chan", "ctx"), P(None, None, "chan"), P("chan", "ctx"))
    return jax.shard_map(
        functools.partial(shards, mesh.shape["ctx"]),
        mesh=mesh, in_specs=in_specs, out_specs=P("chan", "ctx"), check_vma=False,
    )
```

```python
import functools
import math

import jax
import jax.numpy as jnp
import ml_dtypes
import numpy as np
from jax import lax
from jax.experimental import pallas as pl
from jax.experimental.pallas import tpu as pltpu
from jax.sharding import PartitionSpec as P

MESH = pl.DeviceIdType.MESH
LANES = 128
SIDE = 256
TOTAL = SIDE * SIDE
PARTS = 16


def tables():
    k = np.arange(SIDE, dtype=np.float64)

    def cis(a, b, length):
        angle = 2.0 * np.pi * np.fmod(a[:, None] * b[None, :], length) / length
        return np.cos(angle), np.sin(angle)

    cos, sin = cis(k + 0.25, k, SIDE)
    rows = np.concatenate([cos, -sin], axis=1)
    back_rows = np.concatenate([cos.T, -sin.T], axis=1) / TOTAL
    twist = np.stack(cis(k + 0.25, k, TOTAL))
    cos, sin = cis(k, k, SIDE)
    columns = np.block([[cos, -sin], [sin, cos]])
    back_columns = np.block([[cos, sin], [-sin, cos]])
    dft = [rows, back_rows, columns, back_columns]

    steps = SIDE // PARTS
    few = np.arange(steps, dtype=np.float64)
    cos, sin = cis(few + 0.25, few, steps)
    every = np.eye(PARTS)
    rows = np.concatenate([np.kron(every, cos), np.kron(every, -sin)], axis=1)
    back_rows = np.concatenate([np.kron(every, cos.T), np.kron(every, -sin.T)], axis=1) / (steps * SIDE)
    part_twist = np.stack([np.tile(t, (PARTS, 1)) for t in cis(few + 0.25, k, steps * SIDE)])
    dft = np.concatenate(dft + [rows, back_rows], axis=0)
    return dft.astype(ml_dtypes.bfloat16), np.concatenate([twist, part_twist]).astype(np.float32)


def steps_of(n):
    side = math.isqrt(n)
    steps = [(a, b) for a in range(side) for b in range(side) if a or b]
    return sorted(steps, key=lambda step: -sum(min(s, side - s) for s in step))


def kernel(
    n,
    proj_hbm, filt_hbm, taps_hbm, dft_hbm, twist_hbm,
    out,
    proj, filt, taps_ref, dft, twists, gate, stage, q_halo, head, sent, got, e_out, e_in, h_freq,
    load_sem, halo_recv, sent_sem, got_sem, e_recv, column_in,
):
    f32, bf16 = jnp.float32, jnp.bfloat16
    me = lax.axis_index("ctx")
    side = math.isqrt(n)
    my_row, my_column = me // side, lax.rem(me, side)

    def device(step):
        return lax.rem(my_row + step[0], side) * side + lax.rem(my_column + step[1], side)

    steps = steps_of(n)
    mates = [step for step in steps if not (step[0] and step[1])]
    width = filt.shape[1]
    tiles = width // LANES
    half = filt.shape[0] // 2

    barrier = pltpu.get_barrier_semaphore()
    for step in mates:
        pl.semaphore_signal(barrier, inc=1, device_id={"ctx": device(step)}, device_id_type=MESH)
    loads = [
        pltpu.make_async_copy(source, target, load_sem.at[at])
        for at, (source, target) in enumerate([
            (filt_hbm, filt), (taps_hbm, taps_ref), (proj_hbm, proj), (dft_hbm, dft), (twist_hbm, twists),
        ])
    ]
    for load in loads:
        load.start()
    whole = dft.at[0:SIDE], dft.at[SIDE : 2 * SIDE], twists.at[0:2]
    part = dft.at[6 * SIDE : 7 * SIDE], dft.at[7 * SIDE : 8 * SIDE], twists.at[2:4]
    columns, back_columns = dft.at[2 * SIDE : 4 * SIDE], dft.at[4 * SIDE : 6 * SIDE]
    filters, mixes, results = (0, 2), (1, 3), (4, 5)

    def block(ref, at):
        return ref.at[pl.ds(at, 1)]

    def remote(source, target, send_sem, recv_sem, peer):
        return pltpu.make_async_remote_copy(
            src_ref=source, dst_ref=target, send_sem=send_sem, recv_sem=recv_sem,
            device_id={"ctx": peer}, device_id_type=MESH,
        )

    def send(at, chosen):
        for step in chosen:
            peer = device(step)
            remote(block(sent.at[at], peer), block(got.at[at], me), sent_sem, got_sem.at[min(at, 2)], peer).start()

    def send_back(at):
        for step in steps:
            peer = device(step)

            @pl.when(peer != 0)
            def _():
                remote(block(sent.at[at], peer), block(got.at[at], me), sent_sem, got_sem.at[at - 1], peer).start()

        @pl.when(me != 0)
        def _():
            keep(sent.at[at], got.at[at])

    def send_edges(chosen):
        for step in chosen:
            peer = device(step)
            remote(block(e_out, peer), block(e_in, me), sent_sem, e_recv, peer).start()

    def keep(source, target):
        target[pl.ds(me, 1)] = source[pl.ds(me, 1)]

    def others(ref, send_sem, recv_sem):
        part = ref.at[pl.ds(0, n - 1)]
        return remote(part, part, send_sem, recv_sem, me)

    def arrived(at, sem):
        others(got.at[at], got_sem.at[sem], got_sem.at[sem]).wait_recv()

    def spread(value, group, tile_row, parity):
        stage[parity, pl.ds(group * 8 * 16 + tile_row, 8, stride=16), :] = value

    def gathered(target):
        for parity in range(2):
            target[:, :, LANES * parity : LANES * (parity + 1)] = stage[parity].astype(bf16).reshape(n, 16, LANES)

    def place_filter(j):
        def tile_pair(row, carry):
            for parity in range(2):
                at = pl.multiple_of((2 * row + parity) * LANES, LANES)
                value = filt[half * j : half * (j + 1), pl.ds(at, LANES)].astype(f32)
                for group in range(2):
                    spread(value[8 * group : 8 * group + 8], group, row, parity)
            return carry

        lax.fori_loop(0, tiles // 2, tile_pair, 0, unroll=True)
        gathered(sent.at[filters[j]])
        keep(sent.at[filters[j]], got.at[filters[j]])

    diagonal = lax.broadcasted_iota(jnp.int32, (half, 2 * half), 0)
    along = lax.broadcasted_iota(jnp.int32, (half, 2 * half), 1)
    lane = lax.broadcasted_iota(jnp.int32, (half, LANES), 1)
    lag_range, zero = range(3), jnp.zeros((half, LANES), f32)

    def tap(stream, lag, j):
        row = jnp.broadcast_to(taps_ref[stream, lag, :][None, :], (half, 2 * half))
        column = jnp.sum(jnp.where(along == diagonal + half * j, row, 0.0), axis=1, keepdims=True)
        return jnp.broadcast_to(column, (half, LANES))

    def own_tap(stream, lag, j):
        row = jnp.broadcast_to(taps_ref[stream, lag, :][None, :], (half, 2 * half))
        column = jnp.sum(jnp.where(along == me + half * j, row, 0.0), axis=1, keepdims=True)
        return jnp.broadcast_to(column, (half, LANES))

    def rolled(value):
        return value, pltpu.roll(value, 1, 1), pltpu.roll(value, 2, 1)

    def tile_of(stream, at, j):
        start = pl.multiple_of(at * LANES, LANES)
        return rolled(proj[stream, half * j : half * (j + 1), pl.ds(start, LANES)].astype(f32))

    def short(taps, now, before):
        one = jnp.where(lane < 1, before[1], now[1])
        two = jnp.where(lane < 2, before[2], now[2])
        return taps[0] * now[0] + taps[1] * one + taps[2] * two

    def place_mixed(j):
        taps = [[tap(stream, lag, j) for lag in lag_range] for stream in (1, 2)]

        def one_tile(row, parity, now, before):
            value = short(taps[0], now[0], before[0]) * short(taps[1], now[1], before[1])
            for group in range(2):
                spread(value[8 * group : 8 * group + 8], group, row, parity)

        def tile_pair(row, before):
            for parity in range(2):
                now = [tile_of(stream, 2 * row + parity, j) for stream in (1, 2)]
                one_tile(row, parity, now, before)
                before = now
            return before

        lax.fori_loop(0, tiles // 2, tile_pair, [(zero, zero, zero)] * 2, unroll=True)
        gathered(sent.at[mixes[j]])
        keep(sent.at[mixes[j]], got.at[mixes[j]])

    def place_edges():
        edges = zero
        for g in range(4):
            channels = slice(half * (g // 2), half * (g // 2) + half)
            first = proj[1 + g % 2, channels, 0:LANES].astype(f32)
            last = proj[1 + g % 2, channels, width - LANES : width].astype(f32)
            edges = jnp.where((lane >= 32 * g) & (lane < 32 * g + 16), pltpu.roll(first, 32 * g, 1) if g else first, edges)
            edges = jnp.where(
                (lane >= 32 * g + 16) & (lane < 32 * g + 32), pltpu.roll(last, 32 * (g + 1), 1) if g < 3 else last, edges
            )
        e_out[...] = edges[:, None, :]
        keep(e_out, e_in)

    def place_heads():
        edges = e_in[...].reshape(n, LANES)
        earlier = jnp.where(lax.broadcasted_iota(jnp.int32, (n, LANES), 0) < 1, 0.0, pltpu.roll(edges, 1, 0))
        for j in range(2):
            product = None
            for stream in (1, 2):
                g = 2 * j + stream - 1
                now = pltpu.roll(edges, LANES - 32 * g, 1) if g else edges
                one = jnp.where(lane < 1, pltpu.roll(earlier, (2 * LANES - 32 * g - 31) % LANES, 1), pltpu.roll(now, 1, 1))
                two = pltpu.roll(earlier, (2 * LANES - 32 * g - 30) % LANES, 1)
                taps = [own_tap(stream, lag, j) for lag in lag_range]
                value = taps[0] * now + taps[1] * one + taps[2] * two
                product = value if product is None else product * value
            for group in range(2):
                head[j, pl.ds(group * 8 * 16, 8, stride=16), :] = product[8 * group : 8 * group + 8]

    def mixed_of(j):
        at_row = lax.broadcasted_iota(jnp.int32, (SIDE, LANES), 0)
        at_lane = lax.broadcasted_iota(jnp.int32, (SIDE, LANES), 1)
        is_head = (lax.rem(at_row, 16) == 0) & (at_lane < 2)
        value = got[mixes[j]].reshape(SIDE, SIDE)
        even = jnp.where(is_head, head[j], value[:, 0:LANES].astype(f32)).astype(bf16)
        return jnp.concatenate([even, value[:, LANES:SIDE]], axis=1)

    def place_gate(j):
        taps = [tap(0, lag, j) for lag in lag_range]

        def tile(at, before):
            now = tile_of(0, at, j)
            gate[half * j : half * (j + 1), pl.ds(pl.multiple_of(at * LANES, LANES), LANES)] = short(taps, now, before)
            return now

        before = rolled(jnp.where(me > 0, q_halo[half * j : half * (j + 1), :].astype(f32), 0.0))
        lax.fori_loop(0, tiles, tile, before, unroll=True)

    def dot(a, b):
        return jnp.dot(a, b, preferred_element_type=f32)

    def forward(values, of):
        rows, _, twist = of
        values = jnp.concatenate(values, axis=1)
        reals, imags = dot(rows[:, :SIDE], values), dot(rows[:, SIDE:], values)
        cos, sin = twist[0], twist[1]
        turned = []
        for at in range(values.shape[1] // SIDE):
            own = slice(SIDE * at, SIDE * (at + 1))
            real, imag = reals[:, own], imags[:, own]
            turned.append(
                jnp.concatenate([(real * cos + imag * sin).astype(bf16), (imag * cos - real * sin).astype(bf16)], axis=1)
            )
        return dot(jnp.concatenate(turned, axis=0), columns[...])

    def convolved(x, h, of):
        _, back_rows, twist = of
        x_re, x_im, h_re, h_im = x[:, :SIDE], x[:, SIDE:], h[:, :SIDE], h[:, SIDE:]
        product = jnp.concatenate(
            [(x_re * h_re - x_im * h_im).astype(bf16), (x_re * h_im + x_im * h_re).astype(bf16)], axis=1
        )
        values = dot(product, back_columns[...])
        real, imag = values[:, :SIDE], values[:, SIDE:]
        cos, sin = twist[0], twist[1]
        turned = jnp.concatenate(
            [(real * cos - imag * sin).astype(bf16), (imag * cos + real * sin).astype(bf16)], axis=0
        )
        return dot(back_rows[...], turned).astype(bf16).reshape(n, 16, SIDE)

    def filter_of(j):
        return got[filters[j]].reshape(SIDE, SIDE)

    loads[0].wait()
    place_filter(0)
    place_filter(1)
    loads[1].wait()
    loads[2].wait()
    place_edges()
    pl.semaphore_wait(barrier, len(mates))
    for step in mates:
        if step[0]:
            pl.semaphore_signal(
                column_in.at[side - 1 - step[0]], inc=1, device_id={"ctx": device(step)}, device_id_type=MESH
            )
    send_edges(mates)
    send(filters[0], mates)
    place_mixed(0)
    send(mixes[0], mates)
    send(filters[1], [step for step in mates if 2 not in step])
    place_mixed(1)
    send(mixes[1], [step for step in mates if 2 not in step])
    for far in (1, side - 1, 2):
        pl.semaphore_wait(column_in.at[far - 1], 1)
        chosen = [step for step in steps if step[0] == far and step[1]]
        send_edges(chosen)
        send(filters[0], chosen)
        send(mixes[0], chosen)
    chosen = [step for step in steps if step[0] and step[1]]
    send(filters[1], chosen)
    send(mixes[1], chosen)
    send(filters[1], [step for step in mates if 2 in step])
    send(mixes[1], [step for step in mates if 2 in step])
    last = proj.at[0, :, pl.ds(width - LANES, LANES)]
    halo = remote(last, q_halo, sent_sem, halo_recv, lax.rem(me + 1, n))
    halo.start()
    for load in loads[3:]:
        load.wait()

    @pl.when(me == 0)
    def _():
        for j in range(2):
            both = forward([sent[at[j]].reshape(SIDE, SIDE) for at in (mixes, filters)], part)
            got[results[j]] = convolved(both[:SIDE], both[SIDE:], part)

    others(e_in, e_recv, e_recv).wait_recv()
    arrived(filters[0], 0)
    place_heads()
    h_freq[...] = forward([filter_of(0)], whole)
    arrived(mixes[0], 1)
    sent[results[0]] = convolved(forward([mixed_of(0)], whole), h_freq[...], whole)
    send_back(results[0])
    pair = got.at[filters[1] : mixes[1] + 1, 0 : n - 1]
    remote(pair, pair, got_sem.at[2], got_sem.at[2], me).wait_recv()
    both = forward([mixed_of(1), filter_of(1)], whole)
    sent[results[1]] = convolved(both[:SIDE], both[SIDE:], whole)
    send_back(results[1])

    halo.wait_recv()
    place_gate(0)
    place_gate(1)

    for j in range(2):
        @pl.when(me != 0)
        def _():
            arrived(results[j], 3 + j)

        stage[0] = got[results[j], :, :, 0:LANES].astype(f32).reshape(SIDE, LANES)
        stage[1] = got[results[j], :, :, LANES:SIDE].astype(f32).reshape(SIDE, LANES)

        def tile_pair(row, carry):
            for parity in range(2):
                at = pl.multiple_of((2 * row + parity) * LANES, LANES)
                value = jnp.concatenate(
                    [stage[parity, pl.ds(group * 8 * 16 + row, 8, stride=16), :] for group in range(2)], axis=0
                )
                value = value * gate[half * j : half * (j + 1), pl.ds(at, LANES)]
                out[half * j : half * (j + 1), pl.ds(at, LANES)] = value.astype(bf16)
            return carry

        lax.fori_loop(0, tiles // 2, tile_pair, 0, unroll=True)

    halo.wait_send()
    others(e_out, sent_sem, sent_sem).wait_send()

    def all_sent(ref, sem):
        remote(ref, ref, sem, sem, me).wait_send()

    all_sent(sent.at[0:4, 0 : n - 1], sent_sem)

    @pl.when(me == 0)
    def _():
        all_sent(sent.at[4:6, 0 : n - 1], sent_sem)

    @pl.when(me != 0)
    def _():
        all_sent(sent.at[4:6, 0 : n - 2], sent_sem)


def shards(n, projections, short_taps, long_filter):
    channels, width = long_filter.shape
    f32, bf16 = jnp.float32, jnp.bfloat16
    outside = pl.BlockSpec(memory_space=pltpu.HBM)
    inside = pl.BlockSpec(memory_space=pltpu.VMEM)
    edges = pltpu.VMEM((n, 1, LANES), f32)
    parts = pltpu.VMEM((6, n, SIDE // n, SIDE), bf16)
    one = pltpu.SemaphoreType.DMA
    operands = [projections, long_filter, short_taps, *(jnp.asarray(t) for t in tables())]
    return pl.pallas_call(
        functools.partial(kernel, n),
        out_shape=jax.ShapeDtypeStruct((channels, width), bf16),
        in_specs=[outside] * len(operands),
        out_specs=inside,
        scratch_shapes=[
            pltpu.VMEM((3, channels, width), bf16),
            pltpu.VMEM((channels, width), bf16),
            pltpu.VMEM((3, 3, channels), f32),
            pltpu.VMEM((8 * SIDE, 2 * SIDE), bf16),
            pltpu.VMEM((4, SIDE, SIDE), f32),
            pltpu.VMEM((channels, width), f32),
            pltpu.VMEM((2, SIDE, LANES), f32),
            pltpu.VMEM((channels, LANES), bf16),
            pltpu.VMEM((2, SIDE, LANES), f32),
            parts, parts, edges, edges,
            pltpu.VMEM((SIDE, 2 * SIDE), f32),
            pltpu.SemaphoreType.DMA((len(operands),)),
            one, one,
            pltpu.SemaphoreType.DMA((5,)),
            one,
            pltpu.SemaphoreType.REGULAR((math.isqrt(n) - 1,)),
        ],
        compiler_params=pltpu.CompilerParams(
            collective_id=0, has_side_effects=True, vmem_limit_bytes=32 * 1024 * 1024
        ),
        name="long_convolution",
    )(*(pltpu.with_memory_space_constraint(x, pltpu.HBM) for x in operands))


def solution(mesh):
    in_specs = (P(None, "chan", "ctx"), P(None, None, "chan"), P("chan", "ctx"))
    return jax.shard_map(
        functools.partial(shards, mesh.shape["ctx"]),
        mesh=mesh, in_specs=in_specs, out_specs=P("chan", "ctx"), check_vma=False,
    )
```

```python
import functools
import math

import jax
import jax.numpy as jnp
import ml_dtypes
import numpy as np
from jax import lax
from jax.experimental import pallas as pl
from jax.experimental.pallas import tpu as pltpu
from jax.sharding import PartitionSpec as P

MESH = pl.DeviceIdType.MESH
LANES = 128
SIDE = 256
TOTAL = SIDE * SIDE
PARTS = 16


def tables():
    k = np.arange(SIDE, dtype=np.float64)

    def cis(a, b, length):
        angle = 2.0 * np.pi * np.fmod(a[:, None] * b[None, :], length) / length
        return np.cos(angle), np.sin(angle)

    cos, sin = cis(k + 0.25, k, SIDE)
    rows = np.concatenate([cos, -sin], axis=1)
    back_rows = np.concatenate([cos.T, -sin.T], axis=1) / TOTAL
    twist = np.stack(cis(k + 0.25, k, TOTAL))
    cos, sin = cis(k, k, SIDE)
    columns = np.block([[cos, -sin], [sin, cos]])
    back_columns = np.block([[cos, sin], [-sin, cos]])
    dft = [rows, back_rows, columns, back_columns]

    steps = SIDE // PARTS
    few = np.arange(steps, dtype=np.float64)
    cos, sin = cis(few + 0.25, few, steps)
    every = np.eye(PARTS)
    rows = np.concatenate([np.kron(every, cos), np.kron(every, -sin)], axis=1)
    back_rows = np.concatenate([np.kron(every, cos.T), np.kron(every, -sin.T)], axis=1) / (steps * SIDE)
    part_twist = np.stack([np.tile(t, (PARTS, 1)) for t in cis(few + 0.25, k, steps * SIDE)])
    dft = np.concatenate(dft + [rows, back_rows], axis=0)
    return dft.astype(ml_dtypes.bfloat16), np.concatenate([twist, part_twist]).astype(np.float32)


def steps_of(n):
    side = math.isqrt(n)
    steps = [(a, b) for a in range(side) for b in range(side) if a or b]
    return sorted(steps, key=lambda step: -sum(min(s, side - s) for s in step))


def kernel(
    n,
    proj_hbm, filt_hbm, taps_hbm, dft_hbm, twist_hbm,
    out,
    proj, filt, taps_ref, dft, twists, gate, stage, q_halo, head, sent, got, e_out, e_in, h_freq,
    load_sem, halo_send, halo_recv, sent_sem, back_sem, got_sem, e_send, e_recv, column_in,
):
    f32, bf16 = jnp.float32, jnp.bfloat16
    me = lax.axis_index("ctx")
    side = math.isqrt(n)
    my_row, my_column = me // side, lax.rem(me, side)

    def device(step):
        return lax.rem(my_row + step[0], side) * side + lax.rem(my_column + step[1], side)

    steps = steps_of(n)
    beside = [step for step in steps if sum(step) in (1, side - 1) and 0 in step]
    beyond = [step for step in steps if step not in beside]
    mates = [step for step in steps if not (step[0] and step[1])]
    width = filt.shape[1]
    tiles = width // LANES
    half = filt.shape[0] // 2

    barrier = pltpu.get_barrier_semaphore()
    for step in mates:
        pl.semaphore_signal(barrier, inc=1, device_id={"ctx": device(step)}, device_id_type=MESH)
    loads = [
        pltpu.make_async_copy(source, target, load_sem.at[at])
        for at, (source, target) in enumerate([
            (filt_hbm, filt), (taps_hbm, taps_ref), (proj_hbm, proj), (dft_hbm, dft), (twist_hbm, twists),
        ])
    ]
    for load in loads:
        load.start()
    whole = dft.at[0:SIDE], dft.at[SIDE : 2 * SIDE], twists.at[0:2]
    part = dft.at[6 * SIDE : 7 * SIDE], dft.at[7 * SIDE : 8 * SIDE], twists.at[2:4]
    columns, back_columns = dft.at[2 * SIDE : 4 * SIDE], dft.at[4 * SIDE : 6 * SIDE]
    filters, mixes, results = (0, 2), (1, 3), (4, 5)

    def block(ref, at):
        return ref.at[pl.ds(at, 1)]

    def remote(source, target, send_sem, recv_sem, peer):
        return pltpu.make_async_remote_copy(
            src_ref=source, dst_ref=target, send_sem=send_sem, recv_sem=recv_sem,
            device_id={"ctx": peer}, device_id_type=MESH,
        )

    def send(at, chosen):
        for step in chosen:
            peer = device(step)
            remote(block(sent.at[at], peer), block(got.at[at], me), sent_sem, got_sem.at[min(at, 2)], peer).start()

    def send_back(at, chosen):
        for step in chosen:
            peer = device(step)

            @pl.when(peer != 0)
            def _():
                remote(block(sent.at[at], peer), block(got.at[at], me), back_sem, got_sem.at[at - 1], peer).start()

    def send_edges(chosen):
        for step in chosen:
            peer = device(step)
            remote(block(e_out, peer), block(e_in, me), e_send, e_recv, peer).start()

    def keep(source, target):
        target[pl.ds(me, 1)] = source[pl.ds(me, 1)]

    def others(ref, send_sem, recv_sem):
        part = ref.at[pl.ds(0, n - 1)]
        return remote(part, part, send_sem, recv_sem, me)

    def arrived(at, sem):
        others(got.at[at], got_sem.at[sem], got_sem.at[sem]).wait_recv()

    def spread(value, group, tile_row, parity):
        stage[parity, pl.ds(group * 8 * 16 + tile_row, 8, stride=16), :] = value

    def gathered(target):
        for parity in range(2):
            target[:, :, LANES * parity : LANES * (parity + 1)] = stage[parity].astype(bf16).reshape(n, 16, LANES)

    def place_filter(j):
        def tile_pair(row, carry):
            for parity in range(2):
                at = pl.multiple_of((2 * row + parity) * LANES, LANES)
                value = filt[half * j : half * (j + 1), pl.ds(at, LANES)].astype(f32)
                for group in range(2):
                    spread(value[8 * group : 8 * group + 8], group, row, parity)
            return carry

        lax.fori_loop(0, tiles // 2, tile_pair, 0, unroll=True)
        gathered(sent.at[filters[j]])
        keep(sent.at[filters[j]], got.at[filters[j]])

    diagonal = lax.broadcasted_iota(jnp.int32, (half, 2 * half), 0)
    along = lax.broadcasted_iota(jnp.int32, (half, 2 * half), 1)
    lane = lax.broadcasted_iota(jnp.int32, (half, LANES), 1)
    lag_range, zero = range(3), jnp.zeros((half, LANES), f32)

    def tap(stream, lag, j):
        row = jnp.broadcast_to(taps_ref[stream, lag, :][None, :], (half, 2 * half))
        column = jnp.sum(jnp.where(along == diagonal + half * j, row, 0.0), axis=1, keepdims=True)
        return jnp.broadcast_to(column, (half, LANES))

    def own_tap(stream, lag, j):
        row = jnp.broadcast_to(taps_ref[stream, lag, :][None, :], (half, 2 * half))
        column = jnp.sum(jnp.where(along == me + half * j, row, 0.0), axis=1, keepdims=True)
        return jnp.broadcast_to(column, (half, LANES))

    def rolled(value):
        return value, pltpu.roll(value, 1, 1), pltpu.roll(value, 2, 1)

    def tile_of(stream, at, j):
        start = pl.multiple_of(at * LANES, LANES)
        return rolled(proj[stream, half * j : half * (j + 1), pl.ds(start, LANES)].astype(f32))

    def short(taps, now, before):
        one = jnp.where(lane < 1, before[1], now[1])
        two = jnp.where(lane < 2, before[2], now[2])
        return taps[0] * now[0] + taps[1] * one + taps[2] * two

    def place_mixed(j):
        taps = [[tap(stream, lag, j) for lag in lag_range] for stream in (1, 2)]

        def one_tile(row, parity, now, before):
            value = short(taps[0], now[0], before[0]) * short(taps[1], now[1], before[1])
            for group in range(2):
                spread(value[8 * group : 8 * group + 8], group, row, parity)

        def tile_pair(row, before):
            for parity in range(2):
                now = [tile_of(stream, 2 * row + parity, j) for stream in (1, 2)]
                one_tile(row, parity, now, before)
                before = now
            return before

        lax.fori_loop(0, tiles // 2, tile_pair, [(zero, zero, zero)] * 2, unroll=True)
        gathered(sent.at[mixes[j]])
        keep(sent.at[mixes[j]], got.at[mixes[j]])

    def place_edges():
        edges = zero
        for g in range(4):
            channels = slice(half * (g // 2), half * (g // 2) + half)
            first = proj[1 + g % 2, channels, 0:LANES].astype(f32)
            last = proj[1 + g % 2, channels, width - LANES : width].astype(f32)
            edges = jnp.where((lane >= 32 * g) & (lane < 32 * g + 16), pltpu.roll(first, 32 * g, 1) if g else first, edges)
            edges = jnp.where(
                (lane >= 32 * g + 16) & (lane < 32 * g + 32), pltpu.roll(last, 32 * (g + 1), 1) if g < 3 else last, edges
            )
        e_out[...] = edges[:, None, :]
        keep(e_out, e_in)

    def place_heads():
        edges = e_in[...].reshape(n, LANES)
        earlier = jnp.where(lax.broadcasted_iota(jnp.int32, (n, LANES), 0) < 1, 0.0, pltpu.roll(edges, 1, 0))
        for j in range(2):
            product = None
            for stream in (1, 2):
                g = 2 * j + stream - 1
                now = pltpu.roll(edges, LANES - 32 * g, 1) if g else edges
                one = jnp.where(lane < 1, pltpu.roll(earlier, (2 * LANES - 32 * g - 31) % LANES, 1), pltpu.roll(now, 1, 1))
                two = pltpu.roll(earlier, (2 * LANES - 32 * g - 30) % LANES, 1)
                taps = [own_tap(stream, lag, j) for lag in lag_range]
                value = taps[0] * now + taps[1] * one + taps[2] * two
                product = value if product is None else product * value
            for group in range(2):
                head[j, pl.ds(group * 8 * 16, 8, stride=16), :] = product[8 * group : 8 * group + 8]

    def mixed_of(j):
        at_row = lax.broadcasted_iota(jnp.int32, (SIDE, LANES), 0)
        at_lane = lax.broadcasted_iota(jnp.int32, (SIDE, LANES), 1)
        is_head = (lax.rem(at_row, 16) == 0) & (at_lane < 2)
        value = got[mixes[j]].reshape(SIDE, SIDE)
        even = jnp.where(is_head, head[j], value[:, 0:LANES].astype(f32)).astype(bf16)
        return jnp.concatenate([even, value[:, LANES:SIDE]], axis=1)

    def place_gate(j):
        taps = [tap(0, lag, j) for lag in lag_range]

        def tile(at, before):
            now = tile_of(0, at, j)
            gate[half * j : half * (j + 1), pl.ds(pl.multiple_of(at * LANES, LANES), LANES)] = short(taps, now, before)
            return now

        before = rolled(jnp.where(me > 0, q_halo[half * j : half * (j + 1), :].astype(f32), 0.0))
        lax.fori_loop(0, tiles, tile, before, unroll=True)

    def dot(a, b):
        return jnp.dot(a, b, preferred_element_type=f32)

    def forward(values, of):
        rows, _, twist = of
        values = jnp.concatenate(values, axis=1)
        reals, imags = dot(rows[:, :SIDE], values), dot(rows[:, SIDE:], values)
        cos, sin = twist[0], twist[1]
        turned = []
        for at in range(values.shape[1] // SIDE):
            own = slice(SIDE * at, SIDE * (at + 1))
            real, imag = reals[:, own], imags[:, own]
            turned.append(
                jnp.concatenate([(real * cos + imag * sin).astype(bf16), (imag * cos - real * sin).astype(bf16)], axis=1)
            )
        return dot(jnp.concatenate(turned, axis=0), columns[...])

    def convolved(x, h, of):
        _, back_rows, twist = of
        x_re, x_im, h_re, h_im = x[:, :SIDE], x[:, SIDE:], h[:, :SIDE], h[:, SIDE:]
        product = jnp.concatenate(
            [(x_re * h_re - x_im * h_im).astype(bf16), (x_re * h_im + x_im * h_re).astype(bf16)], axis=1
        )
        values = dot(product, back_columns[...])
        real, imag = values[:, :SIDE], values[:, SIDE:]
        cos, sin = twist[0], twist[1]
        turned = jnp.concatenate(
            [(real * cos - imag * sin).astype(bf16), (imag * cos + real * sin).astype(bf16)], axis=0
        )
        return dot(back_rows[...], turned).astype(bf16).reshape(n, 16, SIDE)

    def filter_of(j):
        return got[filters[j]].reshape(SIDE, SIDE)

    loads[0].wait()
    place_filter(0)
    place_filter(1)
    loads[1].wait()
    loads[2].wait()
    place_edges()
    pl.semaphore_wait(barrier, len(mates))
    for step in mates:
        if step[0]:
            pl.semaphore_signal(
                column_in.at[side - 1 - step[0]], inc=1, device_id={"ctx": device(step)}, device_id_type=MESH
            )
    send_edges(mates)
    send(filters[0], mates)
    place_mixed(0)
    send(mixes[0], mates)
    send(filters[1], [step for step in mates if 2 not in step])
    place_mixed(1)
    send(mixes[1], [step for step in mates if 2 not in step])
    for far in (1, side - 1, 2):
        pl.semaphore_wait(column_in.at[far - 1], 1)
        chosen = [step for step in steps if step[0] == far and step[1]]
        send_edges(chosen)
        send(filters[0], chosen)
        send(mixes[0], chosen)
    chosen = [step for step in steps if step[0] and step[1]]
    send(filters[1], chosen)
    send(mixes[1], chosen)
    send(filters[1], [step for step in mates if 2 in step])
    send(mixes[1], [step for step in mates if 2 in step])
    last = proj.at[0, :, pl.ds(width - LANES, LANES)]
    halo = remote(last, q_halo, halo_send, halo_recv, lax.rem(me + 1, n))
    halo.start()
    for load in loads[3:]:
        load.wait()

    @pl.when(me == 0)
    def _():
        for j in range(2):
            both = forward([sent[at[j]].reshape(SIDE, SIDE) for at in (mixes, filters)], part)
            got[results[j]] = convolved(both[:SIDE], both[SIDE:], part)

    others(e_in, e_recv, e_recv).wait_recv()
    arrived(filters[0], 0)
    place_heads()
    h_freq[...] = forward([filter_of(0)], whole)
    arrived(mixes[0], 1)
    sent[results[0]] = convolved(forward([mixed_of(0)], whole), h_freq[...], whole)
    send_back(results[0], beyond)

    @pl.when(me != 0)
    def _():
        keep(sent.at[results[0]], got.at[results[0]])

    pair = got.at[filters[1] : mixes[1] + 1, 0 : n - 1]
    remote(pair, pair, got_sem.at[2], got_sem.at[2], me).wait_recv()
    send_back(results[0], beside)
    both = forward([mixed_of(1), filter_of(1)], whole)
    sent[results[1]] = convolved(both[:SIDE], both[SIDE:], whole)
    send_back(results[1], steps)

    @pl.when(me != 0)
    def _():
        keep(sent.at[results[1]], got.at[results[1]])


    halo.wait_recv()
    place_gate(0)
    place_gate(1)

    for j in range(2):
        @pl.when(me != 0)
        def _():
            arrived(results[j], 3 + j)

        stage[0] = got[results[j], :, :, 0:LANES].astype(f32).reshape(SIDE, LANES)
        stage[1] = got[results[j], :, :, LANES:SIDE].astype(f32).reshape(SIDE, LANES)

        def tile_pair(row, carry):
            for parity in range(2):
                at = pl.multiple_of((2 * row + parity) * LANES, LANES)
                value = jnp.concatenate(
                    [stage[parity, pl.ds(group * 8 * 16 + row, 8, stride=16), :] for group in range(2)], axis=0
                )
                value = value * gate[half * j : half * (j + 1), pl.ds(at, LANES)]
                out[half * j : half * (j + 1), pl.ds(at, LANES)] = value.astype(bf16)
            return carry

        lax.fori_loop(0, tiles // 2, tile_pair, 0, unroll=True)

    halo.wait_send()
    others(e_out, e_send, e_send).wait_send()

    def all_sent(ref, sem):
        remote(ref, ref, sem, sem, me).wait_send()

    all_sent(sent.at[0:4, 0 : n - 1], sent_sem)

    @pl.when(me == 0)
    def _():
        all_sent(sent.at[4:6, 0 : n - 1], back_sem)

    @pl.when(me != 0)
    def _():
        all_sent(sent.at[4:6, 0 : n - 2], back_sem)


def shards(n, projections, short_taps, long_filter):
    channels, width = long_filter.shape
    f32, bf16 = jnp.float32, jnp.bfloat16
    outside = pl.BlockSpec(memory_space=pltpu.HBM)
    inside = pl.BlockSpec(memory_space=pltpu.VMEM)
    edges = pltpu.VMEM((n, 1, LANES), f32)
    parts = pltpu.VMEM((6, n, SIDE // n, SIDE), bf16)
    one = pltpu.SemaphoreType.DMA
    operands = [projections, long_filter, short_taps, *(jnp.asarray(t) for t in tables())]
    return pl.pallas_call(
        functools.partial(kernel, n),
        out_shape=jax.ShapeDtypeStruct((channels, width), bf16),
        in_specs=[outside] * len(operands),
        out_specs=inside,
        scratch_shapes=[
            pltpu.VMEM((3, channels, width), bf16),
            pltpu.VMEM((channels, width), bf16),
            pltpu.VMEM((3, 3, channels), f32),
            pltpu.VMEM((8 * SIDE, 2 * SIDE), bf16),
            pltpu.VMEM((4, SIDE, SIDE), f32),
            pltpu.VMEM((channels, width), f32),
            pltpu.VMEM((2, SIDE, LANES), f32),
            pltpu.VMEM((channels, LANES), bf16),
            pltpu.VMEM((2, SIDE, LANES), f32),
            parts, parts, edges, edges,
            pltpu.VMEM((SIDE, 2 * SIDE), f32),
            pltpu.SemaphoreType.DMA((len(operands),)),
            one, one, one, one,
            pltpu.SemaphoreType.DMA((5,)),
            one, one,
            pltpu.SemaphoreType.REGULAR((math.isqrt(n) - 1,)),
        ],
        compiler_params=pltpu.CompilerParams(
            collective_id=0, has_side_effects=True, vmem_limit_bytes=32 * 1024 * 1024
        ),
        name="long_convolution",
    )(*(pltpu.with_memory_space_constraint(x, pltpu.HBM) for x in operands))


def solution(mesh):
    in_specs = (P(None, "chan", "ctx"), P(None, None, "chan"), P("chan", "ctx"))
    return jax.shard_map(
        functools.partial(shards, mesh.shape["ctx"]),
        mesh=mesh, in_specs=in_specs, out_specs=P("chan", "ctx"), check_vma=False,
    )
```
